32 devices in a mesh: wide: 8 (over z, y), pair: 4 (over x, core).
Axes of the slice: x: 2, y: 2, z: 4, core: 2. Of those that a mesh axis runs over, the one named last changes fastest.
Arguments:
- blocks: bfloat16 [128, 1024, 512], P('pair', 'wide'), may hold values from -6 to 6
- basis_a: bfloat16 [1024, 64], replicated, may hold values from -0.1875 to 0.1875
- basis_b: bfloat16 [512, 64], replicated, may hold values from -0.25 to 0.25
- sketch: bfloat16 [128, 64], P(('pair', 'wide')), may hold values from -6 to 6
Outputs:
- transfer: float32 [4096, 64], P(('wide', 'pair'))
- coefficients: float32 [128, 64], P(('pair', 'wide'))
The draws below stay inside these ranges and needn't reach their ends.
All inputs are finite; a program needn't handle non-finite values.
Results may differ from the reference program's by a relative error of at most 0.0041.
Values may be sent and summed in bfloat16 or wider, within the bound.
No kernel may reach another device: no remote copies, remote signals or barrier semaphores. Data moves between devices by JAX's collectives and lax.ppermute only.
A program may use at most 64 MiB of HBM per device.

```python
import jax
import jax.numpy as jnp
from jax import lax

CA = 1024
CB = 512
RA = 64
RB = 64
K = 64
F = 128


def steps_of(stream_key, extent, pieces, low, top_value):
    loudness = 1.0
    for position, parts in pieces:
        steps = jax.random.uniform(jax.random.fold_in(jax.random.fold_in(stream_key, 6), position), (parts,), jnp.float32, low / len(pieces), top_value / len(pieces))
        loudness = loudness * jnp.repeat(jnp.exp(steps), extent[position] // parts).reshape((-1,) + (1,) * (len(extent) - 1 - position))
    return loudness


def normal_values(stream_key, extent, scale, most, cuts=(), held_as=jnp.bfloat16):
    factor_of = steps_of(stream_key, extent, cuts, -0.22, 0.18) if cuts else 1.0
    values = jax.random.normal(stream_key, extent, jnp.float32) * scale * factor_of
    return jnp.minimum(jnp.maximum(values, -most), most).astype(held_as)


def setup_inputs(seed: int = 0) -> dict:
    streams_of = jax.random.split(jax.random.key(seed), 5)
    blocks = normal_values(streams_of[0], (F, CA, CB), 1.0, 6.0, ((0, 4), (1, 8)))
    basis_a = normal_values(streams_of[1], (CA, RA), CA ** -0.5, 0.1875)
    basis_b = normal_values(streams_of[2], (CB, RB), CB ** -0.5, 0.25)
    sketch = normal_values(streams_of[3], (F, K), 1.0, 6.0, ((0, 32),))
    return {"blocks": blocks, "basis_a": basis_a, "basis_b": basis_b, "sketch": sketch}


def reference(blocks, basis_a, basis_b, sketch):

    def per_fibre(fibre_block):
        narrowed = jnp.dot(fibre_block.astype(jnp.float32), basis_b.astype(jnp.float32), preferred_element_type=jnp.float32).astype(jnp.bfloat16)
        folded = jnp.dot(basis_a.T.astype(jnp.float32), narrowed.astype(jnp.float32), preferred_element_type=jnp.float32).astype(jnp.bfloat16)
        return folded.reshape(RA * RB)
    projected = lax.map(per_fibre, blocks)
    sketched = jnp.dot(projected.T.astype(jnp.float32), sketch.astype(jnp.float32), preferred_element_type=jnp.float32)
    gram = jnp.dot(sketched.T, sketched, precision=lax.Precision.HIGHEST)
    lower = jnp.linalg.cholesky(gram)
    parent = lax.linalg.triangular_solve(lower, sketched, left_side=False, lower=True, transpose_a=True)
    transfer = parent * jnp.sqrt(jnp.float32(RA * RB))
    coefficients = jnp.dot(projected.astype(jnp.float32), parent, precision=lax.Precision.HIGHEST)
    return (transfer, coefficients)
```

```python
import functools

import jax
import jax.numpy as jnp
from jax import lax
from jax.experimental import pallas as pl
from jax.experimental.pallas import tpu as pltpu
from jax.sharding import PartitionSpec as P

F32 = jnp.float32
BF16 = jnp.bfloat16
LANES = 128
SQUARE = 4
CHUNKS = 4
NT = (((1,), (1,)), ((), ()))


def split3(x):
    high = x.astype(BF16)
    rest = x - high.astype(F32)
    middle = rest.astype(BF16)
    low = (rest - middle.astype(F32)).astype(BF16)
    return high, middle, low


def project_kernel(blocks, basis_a, basis_b, sketch, *refs):
    outs = refs[:SQUARE]
    held, rows_a, held_b, held_s, diagonal, wanted, sums, sems = refs[SQUARE:]
    wide = lax.axis_index("wide")
    fibres, rows, columns = blocks.shape
    rank_b = basis_b.shape[1]
    rank_a = basis_a.shape[1]
    pairs = fibres // 2
    quad = 4 * rank_b
    per_chunk = fibres // CHUNKS
    copies = [
        pltpu.make_async_copy(basis_b, held_b, sems.at[CHUNKS]),
        pltpu.make_async_copy(
            basis_a.at[pl.ds(pl.multiple_of(wide * rows, rows), rows), :], rows_a, sems.at[CHUNKS + 1]
        ),
        pltpu.make_async_copy(sketch, held_s, sems.at[CHUNKS + 2]),
    ]
    for c in range(CHUNKS):
        part = pl.ds(c * per_chunk, per_chunk)
        copies.append(pltpu.make_async_copy(blocks.at[part], held.at[part], sems.at[c]))
    for copy in copies:
        copy.start()
    diagonal[...] = jnp.zeros(diagonal.shape, BF16)
    copies[0].wait()
    basis = held_b[...]
    for j in range(4):
        part = [jnp.zeros((columns, LANES), BF16)] * (quad // LANES)
        empty = jnp.zeros((columns, rank_b), BF16)
        both = [basis, empty] if j % 2 == 0 else [empty, basis]
        part[j // 2] = jnp.concatenate(both, axis=1)
        diagonal[pl.ds(j * columns, columns), pl.ds(j // 2 * LANES, LANES)] = part[j // 2]
    copies[1].wait()
    turned = rows_a[...].astype(F32).T
    wanted[...] = turned.reshape(wanted.shape)
    square = lax.rem(wide, SQUARE)
    halves = wanted.shape[0]
    left = jnp.concatenate(
        [wanted[half, square ^ k] for k in range(SQUARE) for half in range(halves)], axis=0
    ).astype(BF16)
    for c in range(CHUNKS):
        copies[3 + c].wait()
        here = held[pl.ds(c * per_chunk, per_chunk)]
        here = here.reshape(per_chunk // 4, 4, rows, columns)
        lhs = jnp.concatenate([here[:, j].reshape(per_chunk // 4 * rows, columns) for j in range(4)], axis=1)
        narrowed = jnp.dot(lhs, diagonal[...], preferred_element_type=F32).astype(BF16)
        for q in range(per_chunk // 4):
            found = jnp.dot(left, narrowed[q * rows : (q + 1) * rows], preferred_element_type=F32)
            for t in range(quad // LANES):
                s = (c * per_chunk // 4 + q) * 2 + t
                sums[pl.ds(s, rank_a, stride=pairs), :] = found[:, t * LANES : (t + 1) * LANES]
    copies[2].wait()
    mine = held_s[...].astype(F32)
    own = mine.shape[0]
    row = lax.broadcasted_iota(jnp.int32, (pairs, LANES), 0)
    tile = jnp.zeros((pairs, LANES), F32)
    for j in range(own // 2):
        line = jnp.concatenate([mine[2 * j : 2 * j + 1], mine[2 * j + 1 : 2 * j + 2]], axis=1)
        tile = jnp.where(row == wide * (own // 2) + j, line, tile)
    count = rank_a // SQUARE
    for k in range(SQUARE):
        found = sums[pl.ds(k * count * pairs, count * pairs), :].reshape(count, pairs, LANES)
        outs[k][pl.ds(0, count)] = found.astype(BF16)
        outs[k][count] = tile.astype(BF16)


def project(blocks, basis_a, basis_b, sketch):
    fibres, rows, columns = blocks.shape
    rank_a = basis_a.shape[1]
    rank_b = basis_b.shape[1]
    pairs = fibres // 2
    wide = lax.axis_size("wide")
    count = rank_a // SQUARE
    out = jax.ShapeDtypeStruct((count + 1, pairs, LANES), BF16)
    vmem = pl.BlockSpec(memory_space=pltpu.VMEM)
    anywhere = pl.BlockSpec(memory_space=pl.ANY)
    return pl.pallas_call(
        project_kernel,
        out_shape=[out] * SQUARE,
        in_specs=[anywhere] * 4,
        out_specs=[vmem] * SQUARE,
        scratch_shapes=[
            pltpu.VMEM(blocks.shape, BF16),
            pltpu.VMEM((rows, rank_a), BF16),
            pltpu.VMEM(basis_b.shape, BF16),
            pltpu.VMEM(sketch.shape, BF16),
            pltpu.VMEM((4 * columns, 4 * rank_b), BF16),
            pltpu.VMEM((wide // SQUARE, SQUARE, rank_a // wide, rows), F32),
            pltpu.VMEM((rank_a * pairs, LANES), F32),
            pltpu.SemaphoreType.DMA((CHUNKS + 3,)),
        ],
        compiler_params=pltpu.CompilerParams(vmem_limit_bytes=32 * 2**20),
        name="project",
    )(blocks, basis_a, basis_b, sketch)


def square_kernel(gathered, moment, own, turned_sketch, held):
    groups, tiles, pairs, _ = gathered.shape
    count = tiles - 1
    rank = LANES // 2
    wide = lax.axis_index("wide")
    pair = lax.axis_index("pair")

    def tile(p):
        return gathered[:, p].reshape(groups * pairs, LANES)

    parts = []
    for m in range(count // 2):
        even, odd = tile(2 * m), tile(2 * m + 1)
        first = jnp.concatenate([even[:, :rank], odd[:, :rank]], axis=1)
        second = jnp.concatenate([even[:, rank:], odd[:, rank:]], axis=1)
        parts.append(jnp.concatenate([first, second], axis=0))
    projected = jnp.concatenate(parts, axis=1)
    rides = tile(count).astype(F32)
    omega = jnp.concatenate([rides[:, :rank], rides[:, rank:]], axis=0).T.astype(BF16)
    turned_sketch[...] = omega
    sketched = jnp.dot(omega, projected, preferred_element_type=F32)
    terms = jnp.concatenate(split3(sketched), axis=0)
    product = lax.dot_general(terms, projected, NT, preferred_element_type=F32)
    columns = omega.shape[0]
    moment[...] = product[:columns] + (product[columns : 2 * columns] + product[2 * columns :])
    for m in range(count // 2):
        held[m] = sketched[:, m * LANES : (m + 1) * LANES]
    own[...] = held[lax.div(wide, SQUARE) * groups + pair]


def square_product(gathered):
    groups, tiles, pairs, _ = gathered.shape
    rank = LANES // 2
    vmem = pl.BlockSpec(memory_space=pltpu.VMEM)
    whole = jax.ShapeDtypeStruct((rank, LANES), F32)
    return pl.pallas_call(
        square_kernel,
        out_shape=[whole, whole, jax.ShapeDtypeStruct((rank, LANES), BF16)],
        in_specs=[vmem],
        out_specs=[vmem] * 3,
        scratch_shapes=[pltpu.VMEM(((tiles - 1) // 2, rank, LANES), F32)],
        compiler_params=pltpu.CompilerParams(vmem_limit_bytes=32 * 2**20),
        name="square_product",
    )(gathered)


def finish_kernel(scale, m0, m1, m2, m3, own, turned_sketch, transfer, coefficients):
    wide = lax.axis_index("wide")
    pair = lax.axis_index("pair")
    moment = (m0[...] + m1[...]) + (m2[...] + m3[...])
    rank, fibres = moment.shape
    terms = jnp.concatenate(split3(moment), axis=0)
    product = lax.dot_general(terms, turned_sketch[...], NT, preferred_element_type=F32)
    gram = product[:rank] + (product[rank : 2 * rank] + product[2 * rank :])
    row = lax.broadcasted_iota(jnp.int32, (rank, rank), 0)
    column = lax.broadcasted_iota(jnp.int32, (rank, rank), 1)
    table = jnp.concatenate([gram, (row == column).astype(F32)], axis=1)
    below = lax.broadcasted_iota(jnp.int32, (8, LANES), 0)
    blocks = [table[8 * b : 8 * b + 8] for b in range(rank // 8)]
    inverse = []
    for j in range(rank):
        b, i = divmod(j, 8)
        line = blocks[b][i : i + 1]
        pivot = line[:, j : j + 1]
        inverse.append(line[:, rank:] * lax.rsqrt(pivot))
        line = line / pivot
        for c in range(b, rank // 8):
            factor = blocks[c][:, j : j + 1]
            if c == b:
                factor = jnp.where(below[:, :1] > i, factor, 0.0)
            blocks[c] = blocks[c] - factor * line
    inverse = jnp.concatenate(inverse, axis=0)
    transfer[...] = scale * lax.dot_general(
        own[...].T, inverse, NT, preferred_element_type=F32, precision=lax.Precision.HIGHEST
    )
    count = coefficients.shape[0]
    groups = lax.axis_size("pair")
    per_group = fibres // groups // 2
    j = lax.broadcasted_iota(jnp.int32, (8, fibres), 0)
    at = lax.rem(j, 2) * (fibres // 2) + pair * per_group + wide * (count // 2) + lax.div(j, 2)
    pick = (lax.broadcasted_iota(jnp.int32, (8, fibres), 1) == at).astype(F32)
    mine = lax.dot_general(pick, moment, NT, preferred_element_type=F32, precision=lax.Precision.HIGHEST)
    found = lax.dot_general(mine, inverse, NT, preferred_element_type=F32, precision=lax.Precision.HIGHEST)
    coefficients[...] = found[:count]


def finish(moments, own, turned_sketch, scale, count):
    rank = own.shape[0]
    vmem = pl.BlockSpec(memory_space=pltpu.VMEM)
    return pl.pallas_call(
        functools.partial(finish_kernel, scale),
        out_shape=[
            jax.ShapeDtypeStruct((own.shape[1], rank), F32),
            jax.ShapeDtypeStruct((count, rank), F32),
        ],
        in_specs=[vmem] * 6,
        out_specs=[vmem] * 2,
        compiler_params=pltpu.CompilerParams(vmem_limit_bytes=32 * 2**20),
        name="finish",
    )(*moments, own, turned_sketch)


def partner(x, k):
    return lax.ppermute(x, "wide", [(i, i ^ k) for i in range(lax.axis_size("wide"))])


def in_squares(blocks, basis_a, basis_b, sketch):
    outs = project(blocks, basis_a, basis_b, sketch)
    got = [partner(outs[k], k) for k in range(1, SQUARE)]
    total = outs[0].astype(F32)
    for term in got:
        total = total + term.astype(F32)
    total = total.astype(BF16)
    other = partner(total, SQUARE)
    total = (total.astype(F32) + other.astype(F32)).astype(BF16)
    gathered = lax.all_gather(total, "pair")
    moment, own, turned_sketch = square_product(gathered)
    moments = [moment] + [partner(moment, k) for k in range(1, SQUARE)]
    scale = float((basis_a.shape[1] * basis_b.shape[1]) ** 0.5)
    return tuple(finish(moments, own, turned_sketch, scale, sketch.shape[0]))


def by_columns(blocks, basis_a, basis_b, sketch):
    rank_a, rank_b = basis_a.shape[1], basis_b.shape[1]
    rows = blocks.shape[1]
    wide, pair = lax.axis_size("wide"), lax.axis_size("pair")
    narrowed = jnp.einsum("fac,cr->far", blocks, basis_b, preferred_element_type=F32).astype(BF16)
    own_rows = lax.dynamic_slice_in_dim(basis_a, lax.axis_index("wide") * rows, rows, 0)
    part = jnp.einsum("ap,far->fpr", own_rows, narrowed, preferred_element_type=F32).astype(BF16)
    fibres = part.shape[0]
    part = part.reshape(fibres, wide * pair, -1).swapaxes(0, 1)
    part = lax.all_to_all(part, ("wide", "pair"), 0, 0, tiled=True)
    part = part.reshape(wide, pair * fibres, -1).astype(F32).sum(0)
    omega = lax.all_gather(sketch, ("pair", "wide"), tiled=True).astype(F32)
    exact = functools.partial(jnp.dot, precision=lax.Precision.HIGHEST)
    own = exact(part.T, omega)
    moment = lax.psum(exact(part, own), ("wide", "pair"))
    lower = jnp.linalg.cholesky(exact(omega.T, moment))
    solve = functools.partial(
        lax.linalg.triangular_solve, lower, left_side=False, lower=True, transpose_a=True
    )
    count = sketch.shape[0]
    mine = lax.dynamic_slice_in_dim(moment, lax.axis_index(("pair", "wide")) * count, count, 0)
    return solve(own) * jnp.sqrt(F32(rank_a * rank_b)), solve(mine)


def solution(mesh):
    placed = (P("pair", "wide", None), P(), P(), P(("pair", "wide"), None))

    def per_device(blocks, basis_a, basis_b, sketch):
        fibres, rows, _ = blocks.shape
        rank_a, rank_b = basis_a.shape[1], basis_b.shape[1]
        wide, pair = lax.axis_size("wide"), lax.axis_size("pair")
        fits = (
            wide == 2 * SQUARE
            and rank_b == LANES // 2
            and sketch.shape[1] == LANES // 2
            and rank_a == 2 * wide * pair
            and rows == LANES
            and fibres * pair == LANES
            and fibres % 32 == 0
        )
        return (in_squares if fits else by_columns)(blocks, basis_a, basis_b, sketch)

    return jax.shard_map(
        per_device,
        mesh=mesh,
        in_specs=placed,
        out_specs=(P(("wide", "pair"), None), P(("pair", "wide"), None)),
        check_vma=False,
    )
```

```python
import functools

import jax
import jax.numpy as jnp
from jax import lax
from jax.experimental import pallas as pl
from jax.experimental.pallas import tpu as pltpu
from jax.sharding import PartitionSpec as P

F32 = jnp.float32
BF16 = jnp.bfloat16
LANES = 128
SQUARE = 4
CHUNKS = 1
GROUP = 8
NT = (((1,), (1,)), ((), ()))


def split3(x):
    high = x.astype(BF16)
    rest = x - high.astype(F32)
    middle = rest.astype(BF16)
    low = (rest - middle.astype(F32)).astype(BF16)
    return high, middle, low


def project_kernel(blocks, basis_a, basis_b, sketch, *refs):
    outs = refs[:SQUARE]
    held, rows_a, held_b, held_s, diagonal, wanted, sums, sems = refs[SQUARE:]
    wide = lax.axis_index("wide")
    fibres, rows, columns = blocks.shape
    rank_b = basis_b.shape[0]
    rank_a = basis_a.shape[0]
    pairs = fibres // 2
    quad = 4 * rank_b
    per_chunk = fibres // CHUNKS
    copies = [
        pltpu.make_async_copy(basis_b, held_b, sems.at[CHUNKS]),
        pltpu.make_async_copy(
            basis_a.at[:, pl.ds(pl.multiple_of(wide * rows, rows), rows)], rows_a, sems.at[CHUNKS + 1]
        ),
        pltpu.make_async_copy(sketch, held_s, sems.at[CHUNKS + 2]),
    ]
    for c in range(CHUNKS):
        part = pl.ds(c * per_chunk, per_chunk)
        copies.append(pltpu.make_async_copy(blocks.at[part], held.at[part], sems.at[c]))
    for copy in copies:
        copy.start()
    diagonal[...] = jnp.zeros(diagonal.shape, BF16)
    copies[0].wait()
    basis = held_b[...].astype(F32).T.astype(BF16)
    for j in range(4):
        part = [jnp.zeros((columns, LANES), BF16)] * (quad // LANES)
        empty = jnp.zeros((columns, rank_b), BF16)
        both = [basis, empty] if j % 2 == 0 else [empty, basis]
        part[j // 2] = jnp.concatenate(both, axis=1)
        diagonal[pl.ds(j * columns, columns), pl.ds(j // 2 * LANES, LANES)] = part[j // 2]
    copies[1].wait()
    wanted[...] = rows_a[...].astype(F32).reshape(wanted.shape)
    square = lax.rem(wide, SQUARE)
    halves = wanted.shape[0]
    left = jnp.concatenate(
        [wanted[half, square ^ k] for k in range(SQUARE) for half in range(halves)], axis=0
    ).astype(BF16)
    for c in range(CHUNKS):
        copies[3 + c].wait()
        here = held[pl.ds(c * per_chunk, per_chunk)]
        here = here.reshape(per_chunk // 4, 4, rows, columns)
        lhs = jnp.concatenate([here[:, j].reshape(per_chunk // 4 * rows, columns) for j in range(4)], axis=1)
        narrowed = jnp.dot(lhs, diagonal[...], preferred_element_type=F32).astype(BF16)
        for q in range(per_chunk // 4):
            found = jnp.dot(left, narrowed[q * rows : (q + 1) * rows], preferred_element_type=F32)
            for t in range(quad // LANES):
                s = (c * per_chunk // 4 + q) * 2 + t
                sums[pl.ds(s, rank_a, stride=pairs), :] = found[:, t * LANES : (t + 1) * LANES]
    copies[2].wait()
    mine = held_s[...].astype(F32)
    own = mine.shape[0]
    row = lax.broadcasted_iota(jnp.int32, (pairs, LANES), 0)
    tile = jnp.zeros((pairs, LANES), F32)
    for j in range(own // 2):
        line = jnp.concatenate([mine[2 * j : 2 * j + 1], mine[2 * j + 1 : 2 * j + 2]], axis=1)
        tile = jnp.where(row == wide * (own // 2) + j, line, tile)
    count = rank_a // SQUARE
    for k in range(SQUARE):
        found = sums[pl.ds(k * count * pairs, count * pairs), :].reshape(count, pairs, LANES)
        outs[k][pl.ds(0, count)] = found.astype(BF16)
        outs[k][count] = tile.astype(BF16)


def project(blocks, basis_a, basis_b, sketch):
    fibres, rows, columns = blocks.shape
    rank_a = basis_a.shape[0]
    rank_b = basis_b.shape[0]
    pairs = fibres // 2
    wide = lax.axis_size("wide")
    count = rank_a // SQUARE
    out = jax.ShapeDtypeStruct((count + 1, pairs, LANES), BF16)
    vmem = pl.BlockSpec(memory_space=pltpu.VMEM)
    outside = pl.BlockSpec(memory_space=pltpu.HBM)
    return pl.pallas_call(
        project_kernel,
        out_shape=[out] * SQUARE,
        in_specs=[outside] * 4,
        out_specs=[vmem] * SQUARE,
        scratch_shapes=[
            pltpu.VMEM(blocks.shape, BF16),
            pltpu.VMEM((rank_a, rows), BF16),
            pltpu.VMEM(basis_b.shape, BF16),
            pltpu.VMEM(sketch.shape, BF16),
            pltpu.VMEM((4 * columns, 4 * rank_b), BF16),
            pltpu.VMEM((wide // SQUARE, SQUARE, rank_a // wide, rows), F32),
            pltpu.VMEM((rank_a * pairs, LANES), F32),
            pltpu.SemaphoreType.DMA((CHUNKS + 3,)),
        ],
        compiler_params=pltpu.CompilerParams(vmem_limit_bytes=58 * 2**20),
        name="project",
    )(blocks, basis_a, basis_b, sketch)


def square_kernel(gathered, moment, own, turned_sketch, held):
    groups, tiles, pairs, _ = gathered.shape
    count = tiles - 1
    rank = LANES // 2
    wide = lax.axis_index("wide")
    pair = lax.axis_index("pair")

    def tile(p):
        return gathered[:, p].reshape(groups * pairs, LANES)

    parts = []
    for m in range(count // 2):
        even, odd = tile(2 * m), tile(2 * m + 1)
        first = jnp.concatenate([even[:, :rank], odd[:, :rank]], axis=1)
        second = jnp.concatenate([even[:, rank:], odd[:, rank:]], axis=1)
        parts.append(jnp.concatenate([first, second], axis=0))
    projected = jnp.concatenate(parts, axis=1)
    rides = tile(count).astype(F32)
    omega = jnp.concatenate([rides[:, :rank], rides[:, rank:]], axis=0).T.astype(BF16)
    turned_sketch[...] = omega
    sketched = jnp.dot(omega, projected, preferred_element_type=F32)
    terms = jnp.concatenate(split3(sketched), axis=0)
    product = lax.dot_general(terms, projected, NT, preferred_element_type=F32)
    columns = omega.shape[0]
    moment[...] = product[:columns] + (product[columns : 2 * columns] + product[2 * columns :])
    for m in range(count // 2):
        held[m] = sketched[:, m * LANES : (m + 1) * LANES]
    own[...] = held[lax.div(wide, SQUARE) * groups + pair]


def square_product(gathered):
    groups, tiles, pairs, _ = gathered.shape
    rank = LANES // 2
    vmem = pl.BlockSpec(memory_space=pltpu.VMEM)
    whole = jax.ShapeDtypeStruct((rank, LANES), F32)
    return pl.pallas_call(
        square_kernel,
        out_shape=[whole, whole, jax.ShapeDtypeStruct((rank, LANES), BF16)],
        in_specs=[vmem],
        out_specs=[vmem] * 3,
        scratch_shapes=[pltpu.VMEM(((tiles - 1) // 2, rank, LANES), F32)],
        compiler_params=pltpu.CompilerParams(vmem_limit_bytes=32 * 2**20),
        name="square_product",
    )(gathered)


def inverse_factor(table):
    rank = table.shape[0]
    tiles = [table[8 * t : 8 * t + 8] for t in range(rank // 8)]
    shape = tiles[0].shape
    below = lax.broadcasted_iota(jnp.int32, shape, 0)
    inverse = []
    for start in range(0, rank, GROUP):
        first, inside = divmod(start, 8)
        last = inside + GROUP == 8
        terms = {
            t: [jnp.broadcast_to(tiles[t][:, start + k : start + k + 1], shape) for k in range(GROUP)]
            for t in range(first, rank // 8)
        }
        lines = [jnp.broadcast_to(tiles[first][inside + k : inside + k + 1], shape) for k in range(GROUP)]
        entry = {
            (k, m): jnp.broadcast_to(terms[first][m][inside + k : inside + k + 1], shape)
            for k in range(GROUP)
            for m in range(k + 1)
        }
        if last:
            del terms[first]
        for k in range(GROUP):
            root = lax.rsqrt(entry[k, k])
            lines[k] = lines[k] * root
            for t in terms:
                terms[t][k] = terms[t][k] * root
            for m in range(k + 1, GROUP):
                entry[m, k] = entry[m, k] * root
            for m in range(k + 1, GROUP):
                for n in range(k + 1, m + 1):
                    entry[m, n] = entry[m, n] - entry[m, k] * entry[n, k]
                lines[m] = lines[m] - entry[m, k] * lines[k]
                for t in terms:
                    terms[t][m] = terms[t][m] - entry[m, k] * terms[t][k]
        for t in terms:
            change = terms[t][0] * lines[0]
            for k in range(1, GROUP):
                change = change + terms[t][k] * lines[k]
            if t == first:
                change = jnp.where(below >= inside + GROUP, change, 0.0)
            tiles[t] = tiles[t] - change
        inverse += [line[:1, rank:] for line in lines]
    return jnp.concatenate(inverse, axis=0)


def finish_kernel(scale, m0, m1, m2, m3, own, turned_sketch, transfer, coefficients):
    wide = lax.axis_index("wide")
    pair = lax.axis_index("pair")
    moment = (m0[...] + m1[...]) + (m2[...] + m3[...])
    rank, fibres = moment.shape
    terms = jnp.concatenate(split3(moment), axis=0)
    product = lax.dot_general(terms, turned_sketch[...], NT, preferred_element_type=F32)
    gram = product[:rank] + (product[rank : 2 * rank] + product[2 * rank :])
    row = lax.broadcasted_iota(jnp.int32, (rank, rank), 0)
    column = lax.broadcasted_iota(jnp.int32, (rank, rank), 1)
    inverse = inverse_factor(jnp.concatenate([gram, (row == column).astype(F32)], axis=1))
    transfer[...] = scale * jnp.dot(
        inverse, own[...], preferred_element_type=F32, precision=lax.Precision.HIGHEST
    )
    count = coefficients.shape[0]
    groups = lax.axis_size("pair")
    per_group = fibres // groups // 2
    j = lax.broadcasted_iota(jnp.int32, (8, fibres), 0)
    at = lax.rem(j, 2) * (fibres // 2) + pair * per_group + wide * (count // 2) + lax.div(j, 2)
    pick = (lax.broadcasted_iota(jnp.int32, (8, fibres), 1) == at).astype(F32)
    mine = lax.dot_general(pick, moment, NT, preferred_element_type=F32, precision=lax.Precision.HIGHEST)
    found = lax.dot_general(mine, inverse, NT, preferred_element_type=F32, precision=lax.Precision.HIGHEST)
    coefficients[...] = found[:count]


def finish(moments, own, turned_sketch, scale, count):
    rank = own.shape[0]
    vmem = pl.BlockSpec(memory_space=pltpu.VMEM)
    return pl.pallas_call(
        functools.partial(finish_kernel, scale),
        out_shape=[
            jax.ShapeDtypeStruct(own.shape, F32),
            jax.ShapeDtypeStruct((count, rank), F32),
        ],
        in_specs=[vmem] * 6,
        out_specs=[vmem] * 2,
        compiler_params=pltpu.CompilerParams(vmem_limit_bytes=32 * 2**20),
        name="finish",
    )(*moments, own, turned_sketch)


def partner(x, k):
    return lax.ppermute(x, "wide", [(i, i ^ k) for i in range(lax.axis_size("wide"))])


def in_squares(blocks, basis_a, basis_b, sketch):
    outs = project(blocks, basis_a.T, basis_b.T, sketch)
    got = [partner(outs[k], k) for k in range(1, SQUARE)]
    total = outs[0].astype(F32)
    for term in got:
        total = total + term.astype(F32)
    total = total.astype(BF16)
    other = partner(total, SQUARE)
    total = (total.astype(F32) + other.astype(F32)).astype(BF16)
    gathered = lax.all_gather(total, "pair")
    moment, own, turned_sketch = square_product(gathered)
    moments = [moment] + [partner(moment, k) for k in range(1, SQUARE)]
    scale = float((basis_a.shape[1] * basis_b.shape[1]) ** 0.5)
    transfer, coefficients = finish(moments, own, turned_sketch, scale, sketch.shape[0])
    return transfer.T, coefficients


def by_columns(blocks, basis_a, basis_b, sketch):
    rank_a, rank_b = basis_a.shape[1], basis_b.shape[1]
    rows = blocks.shape[1]
    wide, pair = lax.axis_size("wide"), lax.axis_size("pair")
    narrowed = jnp.einsum("fac,cr->far", blocks, basis_b, preferred_element_type=F32).astype(BF16)
    own_rows = lax.dynamic_slice_in_dim(basis_a, lax.axis_index("wide") * rows, rows, 0)
    part = jnp.einsum("ap,far->fpr", own_rows, narrowed, preferred_element_type=F32).astype(BF16)
    fibres = part.shape[0]
    part = part.reshape(fibres, wide * pair, -1).swapaxes(0, 1)
    part = lax.all_to_all(part, ("wide", "pair"), 0, 0, tiled=True)
    part = part.reshape(wide, pair * fibres, -1).astype(F32).sum(0)
    omega = lax.all_gather(sketch, ("pair", "wide"), tiled=True).astype(F32)
    exact = functools.partial(jnp.dot, precision=lax.Precision.HIGHEST)
    own = exact(part.T, omega)
    moment = lax.psum(exact(part, own), ("wide", "pair"))
    lower = jnp.linalg.cholesky(exact(omega.T, moment))
    solve = functools.partial(
        lax.linalg.triangular_solve, lower, left_side=False, lower=True, transpose_a=True
    )
    count = sketch.shape[0]
    mine = lax.dynamic_slice_in_dim(moment, lax.axis_index(("pair", "wide")) * count, count, 0)
    return solve(own) * jnp.sqrt(F32(rank_a * rank_b)), solve(mine)


def solution(mesh):
    placed = (P("pair", "wide", None), P(), P(), P(("pair", "wide"), None))

    def per_device(blocks, basis_a, basis_b, sketch):
        fibres, rows, _ = blocks.shape
        rank_a, rank_b = basis_a.shape[1], basis_b.shape[1]
        wide, pair = lax.axis_size("wide"), lax.axis_size("pair")
        fits = (
            wide == 2 * SQUARE
            and rank_b == LANES // 2
            and sketch.shape[1] == LANES // 2
            and rank_a == 2 * wide * pair
            and rows == LANES
            and fibres * pair == LANES
            and fibres % 32 == 0
        )
        return (in_squares if fits else by_columns)(blocks, basis_a, basis_b, sketch)

    return jax.shard_map(
        per_device,
        mesh=mesh,
        in_specs=placed,
        out_specs=(P(("wide", "pair"), None), P(("pair", "wide"), None)),
        check_vma=False,
    )
```

```python
import functools

import jax
import jax.numpy as jnp
from jax import lax
from jax.experimental import pallas as pl
from jax.experimental.pallas import tpu as pltpu
from jax.sharding import PartitionSpec as P

F32 = jnp.float32
BF16 = jnp.bfloat16
LANES = 128
SQUARE = 4
CUTS = (2, 2, 2, 2)
SPLIT = 2
GROUP = 8
NT = (((1,), (1,)), ((), ()))


def split3(x):
    high = x.astype(BF16)
    rest = x - high.astype(F32)
    middle = rest.astype(BF16)
    low = (rest - middle.astype(F32)).astype(BF16)
    return high, middle, low


def project_kernel(blocks, basis_a, basis_b, sketch, *refs):
    outs = refs[:SQUARE]
    held, rows_a, held_b, held_s, diagonal, wanted, sums, sems = refs[SQUARE:]
    wide = lax.axis_index("wide")
    fibres, rows, columns = blocks.shape
    rank_b = basis_b.shape[0]
    rank_a = basis_a.shape[0]
    pairs = fibres // 2
    small = [
        pltpu.make_async_copy(basis_b, held_b, sems.at[0]),
        pltpu.make_async_copy(basis_a.at[:, pl.ds(pl.multiple_of(wide * rows, rows), rows)], rows_a, sems.at[1]),
        pltpu.make_async_copy(sketch, held_s, sems.at[2]),
    ]
    unit = fibres // sum(CUTS)
    parts, begin = [], 0
    for cut in CUTS:
        parts.append((begin, cut * unit))
        begin += cut * unit
    large = [
        pltpu.make_async_copy(blocks.at[pl.ds(at, n)], held.at[pl.ds(at, n)], sems.at[3 + i])
        for i, (at, n) in enumerate(parts)
    ]
    for copy in small + large:
        copy.start()
    small[0].wait()
    basis = held_b[...].astype(F32).T.astype(BF16)
    empty = jnp.zeros_like(basis)
    diagonal[pl.ds(0, columns)] = jnp.concatenate([basis, empty], axis=1)
    diagonal[pl.ds(columns, columns)] = jnp.concatenate([empty, basis], axis=1)
    small[1].wait()
    wanted[...] = rows_a[...].astype(F32).reshape(wanted.shape)
    square = lax.rem(wide, SQUARE)
    halves = wanted.shape[0]
    left = jnp.concatenate(
        [wanted[half, square ^ k] for k in range(SQUARE) for half in range(halves)], axis=0
    ).astype(BF16)

    def narrow(at, n):
        found = []
        for i in range(SPLIT):
            here = held[pl.ds(at + i * n // SPLIT, n // SPLIT)].reshape(n // SPLIT // 2, 2, rows, columns)
            lhs = jnp.concatenate([here[:, j].reshape(-1, columns) for j in range(2)], axis=1)
            found.append(jnp.dot(lhs, diagonal[...], preferred_element_type=F32).astype(BF16))
        return jnp.concatenate(found, axis=0)

    def fold(at, n, narrowed):
        for q in range(n // 4):
            two = [narrowed[(2 * q + t) * rows : (2 * q + t + 1) * rows] for t in range(2)]
            found = jnp.dot(left, jnp.concatenate(two, axis=1), preferred_element_type=F32)
            for t in range(2):
                sums[pl.ds(at // 2 + 2 * q + t, rank_a, stride=pairs), :] = found[:, t * LANES : (t + 1) * LANES]

    late = None
    for copy, (at, n) in zip(large, parts):
        copy.wait()
        narrowed = narrow(at, n)
        if late is not None:
            fold(*late)
        late = (at, n, narrowed)
    fold(*late)
    small[2].wait()
    mine = held_s[...].astype(F32)
    own = mine.shape[0]
    row = lax.broadcasted_iota(jnp.int32, (pairs, LANES), 0)
    tile = jnp.zeros((pairs, LANES), F32)
    for j in range(own // 2):
        line = jnp.concatenate([mine[2 * j : 2 * j + 1], mine[2 * j + 1 : 2 * j + 2]], axis=1)
        tile = jnp.where(row == wide * (own // 2) + j, line, tile)
    count = rank_a // SQUARE
    for k in range(SQUARE):
        found = sums[pl.ds(k * count * pairs, count * pairs), :].reshape(count, pairs, LANES)
        outs[k][pl.ds(0, count)] = found.astype(BF16)
        outs[k][count] = tile.astype(BF16)


def project(blocks, basis_a, basis_b, sketch):
    fibres, rows, columns = blocks.shape
    rank_a = basis_a.shape[0]
    rank_b = basis_b.shape[0]
    pairs = fibres // 2
    wide = lax.axis_size("wide")
    count = rank_a // SQUARE
    out = jax.ShapeDtypeStruct((count + 1, pairs, LANES), BF16)
    vmem = pl.BlockSpec(memory_space=pltpu.VMEM)
    outside = pl.BlockSpec(memory_space=pltpu.HBM)
    return pl.pallas_call(
        project_kernel,
        out_shape=[out] * SQUARE,
        in_specs=[outside] * 4,
        out_specs=[vmem] * SQUARE,
        scratch_shapes=[
            pltpu.VMEM(blocks.shape, BF16),
            pltpu.VMEM((rank_a, rows), BF16),
            pltpu.VMEM(basis_b.shape, BF16),
            pltpu.VMEM(sketch.shape, BF16),
            pltpu.VMEM((2 * columns, 2 * rank_b), BF16),
            pltpu.VMEM((wide // SQUARE, SQUARE, rank_a // wide, rows), F32),
            pltpu.VMEM((rank_a * pairs, LANES), F32),
            pltpu.SemaphoreType.DMA((3 + len(CUTS),)),
        ],
        compiler_params=pltpu.CompilerParams(vmem_limit_bytes=32 * 2**20),
        name="project",
    )(*(pltpu.with_memory_space_constraint(x, pltpu.HBM) for x in (blocks, basis_a, basis_b, sketch)))


def square_kernel(gathered, moment, own, turned_sketch, held):
    groups, tiles, pairs, _ = gathered.shape
    count = tiles - 1
    rank = LANES // 2
    wide = lax.axis_index("wide")
    pair = lax.axis_index("pair")

    def tile(p):
        return gathered[:, p].reshape(groups * pairs, LANES)

    parts = []
    for m in range(count // 2):
        even, odd = tile(2 * m), tile(2 * m + 1)
        first = jnp.concatenate([even[:, :rank], odd[:, :rank]], axis=1)
        second = jnp.concatenate([even[:, rank:], odd[:, rank:]], axis=1)
        parts.append(jnp.concatenate([first, second], axis=0))
    projected = jnp.concatenate(parts, axis=1)
    rides = tile(count).astype(F32)
    omega = jnp.concatenate([rides[:, :rank], rides[:, rank:]], axis=0).T.astype(BF16)
    turned_sketch[...] = omega
    sketched = jnp.dot(omega, projected, preferred_element_type=F32)
    terms = jnp.concatenate(split3(sketched), axis=0)
    product = lax.dot_general(terms, projected, NT, preferred_element_type=F32)
    columns = omega.shape[0]
    moment[...] = product[:columns] + (product[columns : 2 * columns] + product[2 * columns :])
    for m in range(count // 2):
        held[m] = sketched[:, m * LANES : (m + 1) * LANES]
    own[...] = held[lax.div(wide, SQUARE) * groups + pair]


def square_product(gathered):
    groups, tiles, pairs, _ = gathered.shape
    rank = LANES // 2
    vmem = pl.BlockSpec(memory_space=pltpu.VMEM)
    whole = jax.ShapeDtypeStruct((rank, LANES), F32)
    return pl.pallas_call(
        square_kernel,
        out_shape=[whole, whole, jax.ShapeDtypeStruct((rank, LANES), BF16)],
        in_specs=[vmem],
        out_specs=[vmem] * 3,
        scratch_shapes=[pltpu.VMEM(((tiles - 1) // 2, rank, LANES), F32)],
        compiler_params=pltpu.CompilerParams(vmem_limit_bytes=32 * 2**20),
        name="square_product",
    )(gathered)


def inverse_factor(table):
    rank = table.shape[0]
    tiles = [table[8 * t : 8 * t + 8] for t in range(rank // 8)]
    shape = tiles[0].shape
    below = lax.broadcasted_iota(jnp.int32, shape, 0)
    inverse = []
    for start in range(0, rank, GROUP):
        first, inside = divmod(start, 8)
        last = inside + GROUP == 8
        terms = {
            t: [jnp.broadcast_to(tiles[t][:, start + k : start + k + 1], shape) for k in range(GROUP)]
            for t in range(first, rank // 8)
        }
        lines = [jnp.broadcast_to(tiles[first][inside + k : inside + k + 1], shape) for k in range(GROUP)]
        entry = {
            (k, m): jnp.broadcast_to(terms[first][m][inside + k : inside + k + 1], shape)
            for k in range(GROUP)
            for m in range(k + 1)
        }
        if last:
            del terms[first]
        for k in range(GROUP):
            root = lax.rsqrt(entry[k, k])
            lines[k] = lines[k] * root
            for t in terms:
                terms[t][k] = terms[t][k] * root
            for m in range(k + 1, GROUP):
                entry[m, k] = entry[m, k] * root
            for m in range(k + 1, GROUP):
                for n in range(k + 1, m + 1):
                    entry[m, n] = entry[m, n] - entry[m, k] * entry[n, k]
                lines[m] = lines[m] - entry[m, k] * lines[k]
                for t in terms:
                    terms[t][m] = terms[t][m] - entry[m, k] * terms[t][k]
        for t in terms:
            change = terms[t][0] * lines[0]
            for k in range(1, GROUP):
                change = change + terms[t][k] * lines[k]
            if t == first:
                change = jnp.where(below >= inside + GROUP, change, 0.0)
            tiles[t] = tiles[t] - change
        inverse += [line[:1, rank:] for line in lines]
    return jnp.concatenate(inverse, axis=0)


def finish_kernel(scale, m0, m1, m2, m3, own, turned_sketch, transfer, coefficients):
    wide = lax.axis_index("wide")
    pair = lax.axis_index("pair")
    moment = (m0[...] + m1[...]) + (m2[...] + m3[...])
    rank, fibres = moment.shape
    terms = jnp.concatenate(split3(moment), axis=0)
    product = lax.dot_general(terms, turned_sketch[...], NT, preferred_element_type=F32)
    gram = product[:rank] + (product[rank : 2 * rank] + product[2 * rank :])
    row = lax.broadcasted_iota(jnp.int32, (rank, rank), 0)
    column = lax.broadcasted_iota(jnp.int32, (rank, rank), 1)
    inverse = inverse_factor(jnp.concatenate([gram, (row == column).astype(F32)], axis=1))
    transfer[...] = scale * jnp.dot(
        inverse, own[...], preferred_element_type=F32, precision=lax.Precision.HIGHEST
    )
    count = coefficients.shape[0]
    groups = lax.axis_size("pair")
    per_group = fibres // groups // 2
    j = lax.broadcasted_iota(jnp.int32, (8, fibres), 0)
    at = lax.rem(j, 2) * (fibres // 2) + pair * per_group + wide * (count // 2) + lax.div(j, 2)
    pick = (lax.broadcasted_iota(jnp.int32, (8, fibres), 1) == at).astype(F32)
    mine = lax.dot_general(pick, moment, NT, preferred_element_type=F32, precision=lax.Precision.HIGHEST)
    found = lax.dot_general(mine, inverse, NT, preferred_element_type=F32, precision=lax.Precision.HIGHEST)
    coefficients[...] = found[:count]


def finish(moments, own, turned_sketch, scale, count):
    rank = own.shape[0]
    vmem = pl.BlockSpec(memory_space=pltpu.VMEM)
    return pl.pallas_call(
        functools.partial(finish_kernel, scale),
        out_shape=[
            jax.ShapeDtypeStruct(own.shape, F32),
            jax.ShapeDtypeStruct((count, rank), F32),
        ],
        in_specs=[vmem] * 6,
        out_specs=[vmem] * 2,
        compiler_params=pltpu.CompilerParams(vmem_limit_bytes=32 * 2**20),
        name="finish",
    )(*moments, own, turned_sketch)


def partner(x, k):
    return lax.ppermute(x, "wide", [(i, i ^ k) for i in range(lax.axis_size("wide"))])


def in_squares(blocks, basis_a, basis_b, sketch):
    outs = project(blocks, basis_a.T, basis_b.T, sketch)
    got = [partner(outs[k], k) for k in range(1, SQUARE)]
    total = outs[0].astype(F32)
    for term in got:
        total = total + term.astype(F32)
    total = total.astype(BF16)
    other = partner(total, SQUARE)
    total = (total.astype(F32) + other.astype(F32)).astype(BF16)
    gathered = lax.all_gather(total, "pair")
    moment, own, turned_sketch = square_product(gathered)
    moments = [moment] + [partner(moment, k) for k in range(1, SQUARE)]
    scale = float((basis_a.shape[1] * basis_b.shape[1]) ** 0.5)
    transfer, coefficients = finish(moments, own, turned_sketch, scale, sketch.shape[0])
    return transfer.T, coefficients


def by_columns(blocks, basis_a, basis_b, sketch):
    rank_a, rank_b = basis_a.shape[1], basis_b.shape[1]
    rows = blocks.shape[1]
    wide, pair = lax.axis_size("wide"), lax.axis_size("pair")
    narrowed = jnp.einsum("fac,cr->far", blocks, basis_b, preferred_element_type=F32).astype(BF16)
    own_rows = lax.dynamic_slice_in_dim(basis_a, lax.axis_index("wide") * rows, rows, 0)
    part = jnp.einsum("ap,far->fpr", own_rows, narrowed, preferred_element_type=F32).astype(BF16)
    fibres = part.shape[0]
    part = part.reshape(fibres, wide * pair, -1).swapaxes(0, 1)
    part = lax.all_to_all(part, ("wide", "pair"), 0, 0, tiled=True)
    part = part.reshape(wide, pair * fibres, -1).astype(F32).sum(0)
    omega = lax.all_gather(sketch, ("pair", "wide"), tiled=True).astype(F32)
    exact = functools.partial(jnp.dot, precision=lax.Precision.HIGHEST)
    own = exact(part.T, omega)
    moment = lax.psum(exact(part, own), ("wide", "pair"))
    lower = jnp.linalg.cholesky(exact(omega.T, moment))
    solve = functools.partial(
        lax.linalg.triangular_solve, lower, left_side=False, lower=True, transpose_a=True
    )
    count = sketch.shape[0]
    mine = lax.dynamic_slice_in_dim(moment, lax.axis_index(("pair", "wide")) * count, count, 0)
    return solve(own) * jnp.sqrt(F32(rank_a * rank_b)), solve(mine)


def solution(mesh):
    placed = (P("pair", "wide", None), P(), P(), P(("pair", "wide"), None))

    def per_device(blocks, basis_a, basis_b, sketch):
        fibres, rows, _ = blocks.shape
        rank_a, rank_b = basis_a.shape[1], basis_b.shape[1]
        wide, pair = lax.axis_size("wide"), lax.axis_size("pair")
        fits = (
            wide == 2 * SQUARE
            and rank_b == LANES // 2
            and sketch.shape[1] == LANES // 2
            and rank_a == 2 * wide * pair
            and rows == LANES
            and fibres * pair == LANES
            and fibres % 32 == 0
        )
        return (in_squares if fits else by_columns)(blocks, basis_a, basis_b, sketch)

    return jax.shard_map(
        per_device,
        mesh=mesh,
        in_specs=placed,
        out_specs=(P(("wide", "pair"), None), P(("pair", "wide"), None)),
        check_vma=False,
    )
```

```python
import functools

import jax
import jax.numpy as jnp
from jax import lax
from jax.experimental import pallas as pl
from jax.experimental.pallas import tpu as pltpu
from jax.sharding import PartitionSpec as P

F32 = jnp.float32
BF16 = jnp.bfloat16
LANES = 128
SQUARE = 4
CUTS = (2, 2, 2, 2)
SPLIT = 2
FIRST = (3, 2, 1)
SECOND = (1, 2, 3)
GROUP = 8
NT = (((1,), (1,)), ((), ()))


def split3(x):
    high = x.astype(BF16)
    rest = x - high.astype(F32)
    middle = rest.astype(BF16)
    low = (rest - middle.astype(F32)).astype(BF16)
    return high, middle, low


def project_kernel(blocks, basis_a, basis_b, sketch, *refs):
    outs = refs[:SQUARE]
    held, rows_a, held_b, held_s, diagonal, wanted, sums, sems = refs[SQUARE:]
    wide = lax.axis_index("wide")
    fibres, rows, columns = blocks.shape
    rank_b = basis_b.shape[0]
    rank_a = basis_a.shape[0]
    pairs = fibres // 2
    small = [
        pltpu.make_async_copy(basis_b, held_b, sems.at[0]),
        pltpu.make_async_copy(basis_a.at[:, pl.ds(pl.multiple_of(wide * rows, rows), rows)], rows_a, sems.at[1]),
        pltpu.make_async_copy(sketch, held_s, sems.at[2]),
    ]
    unit = fibres // sum(CUTS)
    parts, begin = [], 0
    for cut in CUTS:
        parts.append((begin, cut * unit))
        begin += cut * unit
    large = [
        pltpu.make_async_copy(blocks.at[pl.ds(at, n)], held.at[pl.ds(at, n)], sems.at[3 + i])
        for i, (at, n) in enumerate(parts)
    ]
    for copy in small + large:
        copy.start()
    small[0].wait()
    basis = held_b[...].astype(F32).T.astype(BF16)
    empty = jnp.zeros_like(basis)
    diagonal[pl.ds(0, columns)] = jnp.concatenate([basis, empty], axis=1)
    diagonal[pl.ds(columns, columns)] = jnp.concatenate([empty, basis], axis=1)
    small[1].wait()
    wanted[...] = rows_a[...].astype(F32).reshape(wanted.shape)
    square = lax.rem(wide, SQUARE)
    halves = wanted.shape[0]
    left = jnp.concatenate(
        [wanted[half, square ^ k] for k in range(SQUARE) for half in range(halves)], axis=0
    ).astype(BF16)

    def narrow(at, n):
        found = []
        for i in range(SPLIT):
            here = held[pl.ds(at + i * n // SPLIT, n // SPLIT)].reshape(n // SPLIT // 2, 2, rows, columns)
            lhs = jnp.concatenate([here[:, j].reshape(-1, columns) for j in range(2)], axis=1)
            found.append(jnp.dot(lhs, diagonal[...], preferred_element_type=F32).astype(BF16))
        return jnp.concatenate(found, axis=0)

    def fold(at, n, narrowed):
        for q in range(n // 4):
            two = [narrowed[(2 * q + t) * rows : (2 * q + t + 1) * rows] for t in range(2)]
            found = jnp.dot(left, jnp.concatenate(two, axis=1), preferred_element_type=F32)
            for t in range(2):
                sums[pl.ds(at // 2 + 2 * q + t, rank_a, stride=pairs), :] = found[:, t * LANES : (t + 1) * LANES]

    late = None
    for copy, (at, n) in zip(large, parts):
        copy.wait()
        narrowed = narrow(at, n)
        if late is not None:
            fold(*late)
        late = (at, n, narrowed)
    fold(*late)
    small[2].wait()
    mine = held_s[...].astype(F32)
    own = mine.shape[0]
    row = lax.broadcasted_iota(jnp.int32, (pairs, LANES), 0)
    tile = jnp.zeros((pairs, LANES), F32)
    for j in range(own // 2):
        line = jnp.concatenate([mine[2 * j : 2 * j + 1], mine[2 * j + 1 : 2 * j + 2]], axis=1)
        tile = jnp.where(row == wide * (own // 2) + j, line, tile)
    count = rank_a // SQUARE
    for k in range(SQUARE):
        found = sums[pl.ds(k * count * pairs, count * pairs), :].reshape(count, pairs, LANES)
        outs[k][pl.ds(0, count)] = found.astype(BF16)
        outs[k][count] = tile.astype(BF16)


def project(blocks, basis_a, basis_b, sketch):
    fibres, rows, columns = blocks.shape
    rank_a = basis_a.shape[0]
    rank_b = basis_b.shape[0]
    pairs = fibres // 2
    wide = lax.axis_size("wide")
    count = rank_a // SQUARE
    out = jax.ShapeDtypeStruct((count + 1, pairs, LANES), BF16)
    vmem = pl.BlockSpec(memory_space=pltpu.VMEM)
    outside = pl.BlockSpec(memory_space=pltpu.HBM)
    return pl.pallas_call(
        project_kernel,
        out_shape=[out] * SQUARE,
        in_specs=[outside] * 4,
        out_specs=[vmem] * SQUARE,
        scratch_shapes=[
            pltpu.VMEM(blocks.shape, BF16),
            pltpu.VMEM((rank_a, rows), BF16),
            pltpu.VMEM(basis_b.shape, BF16),
            pltpu.VMEM(sketch.shape, BF16),
            pltpu.VMEM((2 * columns, 2 * rank_b), BF16),
            pltpu.VMEM((wide // SQUARE, SQUARE, rank_a // wide, rows), F32),
            pltpu.VMEM((rank_a * pairs, LANES), F32),
            pltpu.SemaphoreType.DMA((3 + len(CUTS),)),
        ],
        compiler_params=pltpu.CompilerParams(vmem_limit_bytes=32 * 2**20),
        name="project",
    )(*(pltpu.with_memory_space_constraint(x, pltpu.HBM) for x in (blocks, basis_a, basis_b, sketch)))


def square_kernel(gathered, moment, own, turned_sketch, held):
    groups, tiles, pairs, _ = gathered.shape
    count = tiles - 1
    rank = LANES // 2
    wide = lax.axis_index("wide")
    pair = lax.axis_index("pair")

    def tile(p):
        return gathered[:, p].reshape(groups * pairs, LANES)

    parts = []
    for m in range(count // 2):
        even, odd = tile(2 * m), tile(2 * m + 1)
        first = jnp.concatenate([even[:, :rank], odd[:, :rank]], axis=1)
        second = jnp.concatenate([even[:, rank:], odd[:, rank:]], axis=1)
        parts.append(jnp.concatenate([first, second], axis=0))
    projected = jnp.concatenate(parts, axis=1)
    rides = tile(count).astype(F32)
    omega = jnp.concatenate([rides[:, :rank], rides[:, rank:]], axis=0).T.astype(BF16)
    turned_sketch[...] = omega
    sketched = jnp.dot(omega, projected, preferred_element_type=F32)
    terms = jnp.concatenate(split3(sketched), axis=0)
    product = lax.dot_general(terms, projected, NT, preferred_element_type=F32)
    columns = omega.shape[0]
    moment[...] = product[:columns] + (product[columns : 2 * columns] + product[2 * columns :])
    for m in range(count // 2):
        held[m] = sketched[:, m * LANES : (m + 1) * LANES]
    own[...] = held[lax.div(wide, SQUARE) * groups + pair]


def square_product(gathered):
    groups, tiles, pairs, _ = gathered.shape
    rank = LANES // 2
    vmem = pl.BlockSpec(memory_space=pltpu.VMEM)
    whole = jax.ShapeDtypeStruct((rank, LANES), F32)
    return pl.pallas_call(
        square_kernel,
        out_shape=[whole, whole, jax.ShapeDtypeStruct((rank, LANES), BF16)],
        in_specs=[vmem],
        out_specs=[vmem] * 3,
        scratch_shapes=[pltpu.VMEM(((tiles - 1) // 2, rank, LANES), F32)],
        compiler_params=pltpu.CompilerParams(vmem_limit_bytes=32 * 2**20),
        name="square_product",
    )(gathered)


def inverse_factor(table):
    rank = table.shape[0]
    tiles = [table[8 * t : 8 * t + 8] for t in range(rank // 8)]
    shape = tiles[0].shape
    below = lax.broadcasted_iota(jnp.int32, shape, 0)
    inverse = []
    for start in range(0, rank, GROUP):
        first, inside = divmod(start, 8)
        last = inside + GROUP == 8
        terms = {
            t: [jnp.broadcast_to(tiles[t][:, start + k : start + k + 1], shape) for k in range(GROUP)]
            for t in range(first, rank // 8)
        }
        lines = [jnp.broadcast_to(tiles[first][inside + k : inside + k + 1], shape) for k in range(GROUP)]
        entry = {
            (k, m): jnp.broadcast_to(terms[first][m][inside + k : inside + k + 1], shape)
            for k in range(GROUP)
            for m in range(k + 1)
        }
        if last:
            del terms[first]
        for k in range(GROUP):
            root = lax.rsqrt(entry[k, k])
            lines[k] = lines[k] * root
            for t in terms:
                terms[t][k] = terms[t][k] * root
            for m in range(k + 1, GROUP):
                entry[m, k] = entry[m, k] * root
            for m in range(k + 1, GROUP):
                for n in range(k + 1, m + 1):
                    entry[m, n] = entry[m, n] - entry[m, k] * entry[n, k]
                lines[m] = lines[m] - entry[m, k] * lines[k]
                for t in terms:
                    terms[t][m] = terms[t][m] - entry[m, k] * terms[t][k]
        for t in terms:
            change = terms[t][0] * lines[0]
            for k in range(1, GROUP):
                change = change + terms[t][k] * lines[k]
            if t == first:
                change = jnp.where(below >= inside + GROUP, change, 0.0)
            tiles[t] = tiles[t] - change
        inverse += [line[:1, rank:] for line in lines]
    return jnp.concatenate(inverse, axis=0)


def finish_kernel(scale, m0, m1, m2, m3, own, turned_sketch, transfer, coefficients):
    wide = lax.axis_index("wide")
    pair = lax.axis_index("pair")
    moment = (m0[...] + m1[...]) + (m2[...] + m3[...])
    rank, fibres = moment.shape
    terms = jnp.concatenate(split3(moment), axis=0)
    product = lax.dot_general(terms, turned_sketch[...], NT, preferred_element_type=F32)
    gram = product[:rank] + (product[rank : 2 * rank] + product[2 * rank :])
    row = lax.broadcasted_iota(jnp.int32, (rank, rank), 0)
    column = lax.broadcasted_iota(jnp.int32, (rank, rank), 1)
    inverse = inverse_factor(jnp.concatenate([gram, (row == column).astype(F32)], axis=1))
    transfer[...] = scale * jnp.dot(
        inverse, own[...], preferred_element_type=F32, precision=lax.Precision.HIGHEST
    )
    count = coefficients.shape[0]
    groups = lax.axis_size("pair")
    per_group = fibres // groups // 2
    j = lax.broadcasted_iota(jnp.int32, (8, fibres), 0)
    at = lax.rem(j, 2) * (fibres // 2) + pair * per_group + wide * (count // 2) + lax.div(j, 2)
    pick = (lax.broadcasted_iota(jnp.int32, (8, fibres), 1) == at).astype(F32)
    mine = lax.dot_general(pick, moment, NT, preferred_element_type=F32, precision=lax.Precision.HIGHEST)
    found = lax.dot_general(mine, inverse, NT, preferred_element_type=F32, precision=lax.Precision.HIGHEST)
    coefficients[...] = found[:count]


def finish(moments, own, turned_sketch, scale, count):
    rank = own.shape[0]
    vmem = pl.BlockSpec(memory_space=pltpu.VMEM)
    return pl.pallas_call(
        functools.partial(finish_kernel, scale),
        out_shape=[
            jax.ShapeDtypeStruct(own.shape, F32),
            jax.ShapeDtypeStruct((count, rank), F32),
        ],
        in_specs=[vmem] * 6,
        out_specs=[vmem] * 2,
        compiler_params=pltpu.CompilerParams(vmem_limit_bytes=32 * 2**20),
        name="finish",
    )(*moments, own, turned_sketch)


def partner(x, k):
    return lax.ppermute(x, "wide", [(i, i ^ k) for i in range(lax.axis_size("wide"))])


def in_squares(blocks, basis_a, basis_b, sketch):
    outs = project(blocks, basis_a.T, basis_b.T, sketch)
    got = [partner(outs[k], k) for k in FIRST]
    total = outs[0].astype(F32)
    for term in got:
        total = total + term.astype(F32)
    total = total.astype(BF16)
    other = partner(total, SQUARE)
    total = (total.astype(F32) + other.astype(F32)).astype(BF16)
    gathered = lax.all_gather(total, "pair")
    moment, own, turned_sketch = square_product(gathered)
    moments = [moment] + [partner(moment, k) for k in SECOND]
    scale = float((basis_a.shape[1] * basis_b.shape[1]) ** 0.5)
    transfer, coefficients = finish(moments, own, turned_sketch, scale, sketch.shape[0])
    return transfer.T, coefficients


def by_columns(blocks, basis_a, basis_b, sketch):
    rank_a, rank_b = basis_a.shape[1], basis_b.shape[1]
    rows = blocks.shape[1]
    wide, pair = lax.axis_size("wide"), lax.axis_size("pair")
    narrowed = jnp.einsum("fac,cr->far", blocks, basis_b, preferred_element_type=F32).astype(BF16)
    own_rows = lax.dynamic_slice_in_dim(basis_a, lax.axis_index("wide") * rows, rows, 0)
    part = jnp.einsum("ap,far->fpr", own_rows, narrowed, preferred_element_type=F32).astype(BF16)
    fibres = part.shape[0]
    part = part.reshape(fibres, wide * pair, -1).swapaxes(0, 1)
    part = lax.all_to_all(part, ("wide", "pair"), 0, 0, tiled=True)
    part = part.reshape(wide, pair * fibres, -1).astype(F32).sum(0)
    omega = lax.all_gather(sketch, ("pair", "wide"), tiled=True).astype(F32)
    exact = functools.partial(jnp.dot, precision=lax.Precision.HIGHEST)
    own = exact(part.T, omega)
    moment = lax.psum(exact(part, own), ("wide", "pair"))
    lower = jnp.linalg.cholesky(exact(omega.T, moment))
    solve = functools.partial(
        lax.linalg.triangular_solve, lower, left_side=False, lower=True, transpose_a=True
    )
    count = sketch.shape[0]
    mine = lax.dynamic_slice_in_dim(moment, lax.axis_index(("pair", "wide")) * count, count, 0)
    return solve(own) * jnp.sqrt(F32(rank_a * rank_b)), solve(mine)


def solution(mesh):
    placed = (P("pair", "wide", None), P(), P(), P(("pair", "wide"), None))

    def per_device(blocks, basis_a, basis_b, sketch):
        fibres, rows, _ = blocks.shape
        rank_a, rank_b = basis_a.shape[1], basis_b.shape[1]
        wide, pair = lax.axis_size("wide"), lax.axis_size("pair")
        fits = (
            wide == 2 * SQUARE
            and rank_b == LANES // 2
            and sketch.shape[1] == LANES // 2
            and rank_a == 2 * wide * pair
            and rows == LANES
            and fibres * pair == LANES
            and fibres % 32 == 0
        )
        return (in_squares if fits else by_columns)(blocks, basis_a, basis_b, sketch)

    return jax.shard_map(
        per_device,
        mesh=mesh,
        in_specs=placed,
        out_specs=(P(("wide", "pair"), None), P(("pair", "wide"), None)),
        check_vma=False,
    )
```

```python
import functools

import jax
import jax.numpy as jnp
from jax import lax
from jax.experimental import pallas as pl
from jax.experimental.pallas import tpu as pltpu
from jax.sharding import PartitionSpec as P

F32 = jnp.float32
BF16 = jnp.bfloat16
LANES = 128
SQUARE = 4
CUTS = (2, 2, 2, 2)
SPLIT = 2
FIRST = (3, 2, 1)
SECOND = (1, 2, 3)
ACROSS = (3, 2, 1)
CROSS = 1
GROUP = 8
NT = (((1,), (1,)), ((), ()))


def split3(x):
    high = x.astype(BF16)
    rest = x - high.astype(F32)
    middle = rest.astype(BF16)
    low = (rest - middle.astype(F32)).astype(BF16)
    return high, middle, low


def project_kernel(blocks, basis_a, basis_b, sketch, *refs):
    outs = refs[:SQUARE]
    held, rows_a, held_b, held_s, diagonal, wanted, sums, sems = refs[SQUARE:]
    wide = lax.axis_index("wide")
    fibres, rows, columns = blocks.shape
    rank_b = basis_b.shape[0]
    rank_a = basis_a.shape[0]
    pairs = fibres // 2
    small = [
        pltpu.make_async_copy(basis_b, held_b, sems.at[0]),
        pltpu.make_async_copy(basis_a.at[:, pl.ds(pl.multiple_of(wide * rows, rows), rows)], rows_a, sems.at[1]),
        pltpu.make_async_copy(sketch, held_s, sems.at[2]),
    ]
    unit = fibres // sum(CUTS)
    parts, begin = [], 0
    for cut in CUTS:
        parts.append((begin, cut * unit))
        begin += cut * unit
    large = [
        pltpu.make_async_copy(blocks.at[pl.ds(at, n)], held.at[pl.ds(at, n)], sems.at[3 + i])
        for i, (at, n) in enumerate(parts)
    ]
    for copy in small + large:
        copy.start()
    small[0].wait()
    basis = held_b[...].astype(F32).T.astype(BF16)
    empty = jnp.zeros_like(basis)
    diagonal[pl.ds(0, columns)] = jnp.concatenate([basis, empty], axis=1)
    diagonal[pl.ds(columns, columns)] = jnp.concatenate([empty, basis], axis=1)
    small[1].wait()
    wanted[...] = rows_a[...].astype(F32).reshape(wanted.shape)
    square = lax.rem(wide, SQUARE)
    halves = wanted.shape[0]
    left = jnp.concatenate(
        [wanted[half, square ^ k] for k in range(SQUARE) for half in range(halves)], axis=0
    ).astype(BF16)

    def narrow(at, n):
        found = []
        for i in range(SPLIT):
            here = held[pl.ds(at + i * n // SPLIT, n // SPLIT)].reshape(n // SPLIT // 2, 2, rows, columns)
            lhs = jnp.concatenate([here[:, j].reshape(-1, columns) for j in range(2)], axis=1)
            found.append(jnp.dot(lhs, diagonal[...], preferred_element_type=F32).astype(BF16))
        return jnp.concatenate(found, axis=0)

    def fold(at, n, narrowed):
        for q in range(n // 4):
            two = [narrowed[(2 * q + t) * rows : (2 * q + t + 1) * rows] for t in range(2)]
            found = jnp.dot(left, jnp.concatenate(two, axis=1), preferred_element_type=F32)
            for t in range(2):
                sums[pl.ds(at // 2 + 2 * q + t, rank_a, stride=pairs), :] = found[:, t * LANES : (t + 1) * LANES]

    late = None
    for copy, (at, n) in zip(large, parts):
        copy.wait()
        narrowed = narrow(at, n)
        if late is not None:
            fold(*late)
        late = (at, n, narrowed)
    fold(*late)
    small[2].wait()
    mine = held_s[...].astype(F32)
    own = mine.shape[0]
    row = lax.broadcasted_iota(jnp.int32, (pairs, LANES), 0)
    tile = jnp.zeros((pairs, LANES), F32)
    for j in range(own // 2):
        line = jnp.concatenate([mine[2 * j : 2 * j + 1], mine[2 * j + 1 : 2 * j + 2]], axis=1)
        tile = jnp.where(row == wide * (own // 2) + j, line, tile)
    count = rank_a // SQUARE
    for k in range(SQUARE):
        found = sums[pl.ds(k * count * pairs, count * pairs), :].reshape(count, pairs, LANES)
        outs[k][pl.ds(0, count)] = found.astype(BF16)
        outs[k][count] = tile.astype(BF16)


def project(blocks, basis_a, basis_b, sketch):
    fibres, rows, columns = blocks.shape
    rank_a = basis_a.shape[0]
    rank_b = basis_b.shape[0]
    pairs = fibres // 2
    wide = lax.axis_size("wide")
    count = rank_a // SQUARE
    out = jax.ShapeDtypeStruct((count + 1, pairs, LANES), BF16)
    vmem = pl.BlockSpec(memory_space=pltpu.VMEM)
    outside = pl.BlockSpec(memory_space=pltpu.HBM)
    return pl.pallas_call(
        project_kernel,
        out_shape=[out] * SQUARE,
        in_specs=[outside] * 4,
        out_specs=[vmem] * SQUARE,
        scratch_shapes=[
            pltpu.VMEM(blocks.shape, BF16),
            pltpu.VMEM((rank_a, rows), BF16),
            pltpu.VMEM(basis_b.shape, BF16),
            pltpu.VMEM(sketch.shape, BF16),
            pltpu.VMEM((2 * columns, 2 * rank_b), BF16),
            pltpu.VMEM((wide // SQUARE, SQUARE, rank_a // wide, rows), F32),
            pltpu.VMEM((rank_a * pairs, LANES), F32),
            pltpu.SemaphoreType.DMA((3 + len(CUTS),)),
        ],
        compiler_params=pltpu.CompilerParams(vmem_limit_bytes=32 * 2**20),
        name="project",
    )(*(pltpu.with_memory_space_constraint(x, pltpu.HBM) for x in (blocks, basis_a, basis_b, sketch)))


def square_kernel(*refs):
    groups = len(refs) - 5
    moment, own, turned_sketch, gathered, held = refs[groups:]
    _, tiles, pairs, _ = gathered.shape
    count = tiles - 1
    rank = LANES // 2
    wide = lax.axis_index("wide")
    pair = lax.axis_index("pair")
    for k in range(groups):
        gathered[pair ^ k] = refs[k][...]

    def tile(p):
        return gathered[:, p].reshape(groups * pairs, LANES)

    parts = []
    for m in range(count // 2):
        even, odd = tile(2 * m), tile(2 * m + 1)
        first = jnp.concatenate([even[:, :rank], odd[:, :rank]], axis=1)
        second = jnp.concatenate([even[:, rank:], odd[:, rank:]], axis=1)
        parts.append(jnp.concatenate([first, second], axis=0))
    projected = jnp.concatenate(parts, axis=1)
    rides = tile(count).astype(F32)
    omega = jnp.concatenate([rides[:, :rank], rides[:, rank:]], axis=0).T.astype(BF16)
    turned_sketch[...] = omega
    sketched = jnp.dot(omega, projected, preferred_element_type=F32)
    terms = jnp.concatenate(split3(sketched), axis=0)
    product = lax.dot_general(terms, projected, NT, preferred_element_type=F32)
    columns = omega.shape[0]
    moment[...] = product[:columns] + (product[columns : 2 * columns] + product[2 * columns :])
    for m in range(count // 2):
        held[m] = sketched[:, m * LANES : (m + 1) * LANES]
    own[...] = held[lax.div(wide, SQUARE) * groups + pair]


def square_product(*groups):
    tiles, pairs, _ = groups[0].shape
    rank = LANES // 2
    vmem = pl.BlockSpec(memory_space=pltpu.VMEM)
    whole = jax.ShapeDtypeStruct((rank, LANES), F32)
    return pl.pallas_call(
        square_kernel,
        out_shape=[whole, whole, jax.ShapeDtypeStruct((rank, LANES), BF16)],
        in_specs=[vmem] * len(groups),
        out_specs=[vmem] * 3,
        scratch_shapes=[
            pltpu.VMEM((len(groups),) + groups[0].shape, BF16),
            pltpu.VMEM(((tiles - 1) // 2, rank, LANES), F32),
        ],
        compiler_params=pltpu.CompilerParams(vmem_limit_bytes=32 * 2**20),
        name="square_product",
    )(*groups)


def inverse_factor(table):
    rank = table.shape[0]
    tiles = [table[8 * t : 8 * t + 8] for t in range(rank // 8)]
    shape = tiles[0].shape
    below = lax.broadcasted_iota(jnp.int32, shape, 0)
    inverse = []
    for start in range(0, rank, GROUP):
        first, inside = divmod(start, 8)
        last = inside + GROUP == 8
        terms = {
            t: [jnp.broadcast_to(tiles[t][:, start + k : start + k + 1], shape) for k in range(GROUP)]
            for t in range(first, rank // 8)
        }
        lines = [jnp.broadcast_to(tiles[first][inside + k : inside + k + 1], shape) for k in range(GROUP)]
        entry = {
            (k, m): jnp.broadcast_to(terms[first][m][inside + k : inside + k + 1], shape)
            for k in range(GROUP)
            for m in range(k + 1)
        }
        if last:
            del terms[first]
        for k in range(GROUP):
            root = lax.rsqrt(entry[k, k])
            lines[k] = lines[k] * root
            for t in terms:
                terms[t][k] = terms[t][k] * root
            for m in range(k + 1, GROUP):
                entry[m, k] = entry[m, k] * root
            for m in range(k + 1, GROUP):
                for n in range(k + 1, m + 1):
                    entry[m, n] = entry[m, n] - entry[m, k] * entry[n, k]
                lines[m] = lines[m] - entry[m, k] * lines[k]
                for t in terms:
                    terms[t][m] = terms[t][m] - entry[m, k] * terms[t][k]
        for t in terms:
            change = terms[t][0] * lines[0]
            for k in range(1, GROUP):
                change = change + terms[t][k] * lines[k]
            if t == first:
                change = jnp.where(below >= inside + GROUP, change, 0.0)
            tiles[t] = tiles[t] - change
        inverse += [line[:1, rank:] for line in lines]
    return jnp.concatenate(inverse, axis=0)


def finish_kernel(scale, m0, m1, m2, m3, own, turned_sketch, transfer, coefficients):
    wide = lax.axis_index("wide")
    pair = lax.axis_index("pair")
    moment = (m0[...] + m1[...]) + (m2[...] + m3[...])
    rank, fibres = moment.shape
    terms = jnp.concatenate(split3(moment), axis=0)
    product = lax.dot_general(terms, turned_sketch[...], NT, preferred_element_type=F32)
    gram = product[:rank] + (product[rank : 2 * rank] + product[2 * rank :])
    row = lax.broadcasted_iota(jnp.int32, (rank, rank), 0)
    column = lax.broadcasted_iota(jnp.int32, (rank, rank), 1)
    inverse = inverse_factor(jnp.concatenate([gram, (row == column).astype(F32)], axis=1))
    transfer[...] = scale * jnp.dot(
        inverse, own[...], preferred_element_type=F32, precision=lax.Precision.HIGH
    )
    count = coefficients.shape[0]
    groups = lax.axis_size("pair")
    per_group = fibres // groups // 2
    j = lax.broadcasted_iota(jnp.int32, (8, fibres), 0)
    at = lax.rem(j, 2) * (fibres // 2) + pair * per_group + wide * (count // 2) + lax.div(j, 2)
    pick = (lax.broadcasted_iota(jnp.int32, (8, fibres), 1) == at).astype(F32)
    mine = lax.dot_general(pick, moment, NT, preferred_element_type=F32, precision=lax.Precision.HIGHEST)
    found = lax.dot_general(mine, inverse, NT, preferred_element_type=F32, precision=lax.Precision.HIGH)
    coefficients[...] = found[:count]


def finish(moments, own, turned_sketch, scale, count):
    rank = own.shape[0]
    vmem = pl.BlockSpec(memory_space=pltpu.VMEM)
    return pl.pallas_call(
        functools.partial(finish_kernel, scale),
        out_shape=[
            jax.ShapeDtypeStruct(own.shape, F32),
            jax.ShapeDtypeStruct((count, rank), F32),
        ],
        in_specs=[vmem] * 6,
        out_specs=[vmem] * 2,
        compiler_params=pltpu.CompilerParams(vmem_limit_bytes=32 * 2**20),
        name="finish",
    )(*moments, own, turned_sketch)


def partner(x, k):
    return lax.ppermute(x, "wide", [(i, i ^ k) for i in range(lax.axis_size("wide"))])


def beside(x, k, j):
    wide, pair = lax.axis_size("wide"), lax.axis_size("pair")
    pairs = [(i * pair + g, (i ^ k) * pair + (g ^ j)) for i in range(wide) for g in range(pair)]
    return lax.ppermute(x, ("wide", "pair"), pairs)


def in_squares(blocks, basis_a, basis_b, sketch):
    outs = project(blocks, basis_a.T, basis_b.T, sketch)
    got = [partner(outs[k], k) for k in FIRST]
    total = outs[0].astype(F32)
    for term in got:
        total = total + term.astype(F32)
    total = total.astype(BF16)
    other = partner(total, SQUARE)
    total = (total.astype(F32) + other.astype(F32)).astype(BF16)
    groups = {0: total} | {k: beside(total, 0, k) for k in ACROSS}
    moment, own, turned_sketch = square_product(*(groups[k] for k in range(len(groups))))
    moments = [moment] + [beside(moment, k, CROSS) for k in SECOND]
    scale = float((basis_a.shape[1] * basis_b.shape[1]) ** 0.5)
    transfer, coefficients = finish(moments, own, turned_sketch, scale, sketch.shape[0])
    return transfer.T, coefficients


def by_columns(blocks, basis_a, basis_b, sketch):
    rank_a, rank_b = basis_a.shape[1], basis_b.shape[1]
    rows = blocks.shape[1]
    wide, pair = lax.axis_size("wide"), lax.axis_size("pair")
    narrowed = jnp.einsum("fac,cr->far", blocks, basis_b, preferred_element_type=F32).astype(BF16)
    own_rows = lax.dynamic_slice_in_dim(basis_a, lax.axis_index("wide") * rows, rows, 0)
    part = jnp.einsum("ap,far->fpr", own_rows, narrowed, preferred_element_type=F32).astype(BF16)
    fibres = part.shape[0]
    part = part.reshape(fibres, wide * pair, -1).swapaxes(0, 1)
    part = lax.all_to_all(part, ("wide", "pair"), 0, 0, tiled=True)
    part = part.reshape(wide, pair * fibres, -1).astype(F32).sum(0)
    omega = lax.all_gather(sketch, ("pair", "wide"), tiled=True).astype(F32)
    exact = functools.partial(jnp.dot, precision=lax.Precision.HIGHEST)
    own = exact(part.T, omega)
    moment = lax.psum(exact(part, own), ("wide", "pair"))
    lower = jnp.linalg.cholesky(exact(omega.T, moment))
    solve = functools.partial(
        lax.linalg.triangular_solve, lower, left_side=False, lower=True, transpose_a=True
    )
    count = sketch.shape[0]
    mine = lax.dynamic_slice_in_dim(moment, lax.axis_index(("pair", "wide")) * count, count, 0)
    return solve(own) * jnp.sqrt(F32(rank_a * rank_b)), solve(mine)


def solution(mesh):
    placed = (P("pair", "wide", None), P(), P(), P(("pair", "wide"), None))

    def per_device(blocks, basis_a, basis_b, sketch):
        fibres, rows, _ = blocks.shape
        rank_a, rank_b = basis_a.shape[1], basis_b.shape[1]
        wide, pair = lax.axis_size("wide"), lax.axis_size("pair")
        fits = (
            wide == 2 * SQUARE
            and rank_b == LANES // 2
            and sketch.shape[1] == LANES // 2
            and rank_a == 2 * wide * pair
            and rows == LANES
            and fibres * pair == LANES
            and fibres % 32 == 0
        )
        return (in_squares if fits else by_columns)(blocks, basis_a, basis_b, sketch)

    return jax.shard_map(
        per_device,
        mesh=mesh,
        in_specs=placed,
        out_specs=(P(("wide", "pair"), None), P(("pair", "wide"), None)),
        check_vma=False,
    )
```

```python
import functools

import jax
import jax.numpy as jnp
from jax import lax
from jax.experimental import pallas as pl
from jax.experimental.pallas import tpu as pltpu
from jax.sharding import PartitionSpec as P

F32 = jnp.float32
BF16 = jnp.bfloat16
LANES = 128
SQUARE = 4
CUTS = (2, 2, 2, 2)
SPLIT = 2
FIRST = (3, 2, 1)
SECOND = (1, 2, 3)
GROUP = 8
NT = (((1,), (1,)), ((), ()))


def split3(x):
    high = x.astype(BF16)
    rest = x - high.astype(F32)
    middle = rest.astype(BF16)
    low = (rest - middle.astype(F32)).astype(BF16)
    return high, middle, low


def project_kernel(blocks, basis_a, basis_b, sketch, *refs):
    outs = refs[:SQUARE]
    held, rows_a, held_b, held_s, diagonal, wanted, sums, sems = refs[SQUARE:]
    wide = lax.axis_index("wide")
    fibres, rows, columns = blocks.shape
    rank_b = basis_b.shape[0]
    rank_a = basis_a.shape[0]
    pairs = fibres // 2
    small = [
        pltpu.make_async_copy(basis_b, held_b, sems.at[0]),
        pltpu.make_async_copy(basis_a.at[:, pl.ds(pl.multiple_of(wide * rows, rows), rows)], rows_a, sems.at[1]),
        pltpu.make_async_copy(sketch, held_s, sems.at[2]),
    ]
    unit = fibres // sum(CUTS)
    parts, begin = [], 0
    for cut in CUTS:
        parts.append((begin, cut * unit))
        begin += cut * unit
    large = [
        pltpu.make_async_copy(blocks.at[pl.ds(at, n)], held.at[pl.ds(at, n)], sems.at[3 + i])
        for i, (at, n) in enumerate(parts)
    ]
    for copy in small + large:
        copy.start()
    small[0].wait()
    basis = held_b[...].astype(F32).T.astype(BF16)
    empty = jnp.zeros_like(basis)
    diagonal[pl.ds(0, columns)] = jnp.concatenate([basis, empty], axis=1)
    diagonal[pl.ds(columns, columns)] = jnp.concatenate([empty, basis], axis=1)
    small[1].wait()
    wanted[...] = rows_a[...].astype(F32).reshape(wanted.shape)
    square = lax.rem(wide, SQUARE)
    halves = wanted.shape[0]
    left = jnp.concatenate(
        [wanted[half, square ^ k] for k in range(SQUARE) for half in range(halves)], axis=0
    ).astype(BF16)

    def narrow(at, n):
        found = []
        for i in range(SPLIT):
            here = held[pl.ds(at + i * n // SPLIT, n // SPLIT)].reshape(n // SPLIT // 2, 2, rows, columns)
            lhs = jnp.concatenate([here[:, j].reshape(-1, columns) for j in range(2)], axis=1)
            found.append(jnp.dot(lhs, diagonal[...], preferred_element_type=F32).astype(BF16))
        return jnp.concatenate(found, axis=0)

    def fold(at, n, narrowed):
        for q in range(n // 4):
            two = [narrowed[(2 * q + t) * rows : (2 * q + t + 1) * rows] for t in range(2)]
            found = jnp.dot(left, jnp.concatenate(two, axis=1), preferred_element_type=F32)
            for t in range(2):
                sums[pl.ds(at // 2 + 2 * q + t, rank_a, stride=pairs), :] = found[:, t * LANES : (t + 1) * LANES]

    late = None
    for copy, (at, n) in zip(large, parts):
        copy.wait()
        narrowed = narrow(at, n)
        if late is not None:
            fold(*late)
        late = (at, n, narrowed)
    fold(*late)
    small[2].wait()
    mine = held_s[...].astype(F32)
    own = mine.shape[0]
    row = lax.broadcasted_iota(jnp.int32, (pairs, LANES), 0)
    tile = jnp.zeros((pairs, LANES), F32)
    for j in range(own // 2):
        line = jnp.concatenate([mine[2 * j : 2 * j + 1], mine[2 * j + 1 : 2 * j + 2]], axis=1)
        tile = jnp.where(row == wide * (own // 2) + j, line, tile)
    count = rank_a // SQUARE
    for k in range(SQUARE):
        found = sums[pl.ds(k * count * pairs, count * pairs), :].reshape(count, pairs, LANES)
        outs[k][pl.ds(0, count)] = found.astype(BF16)
        outs[k][count] = tile.astype(BF16)


def project(blocks, basis_a, basis_b, sketch):
    fibres, rows, columns = blocks.shape
    rank_a = basis_a.shape[0]
    rank_b = basis_b.shape[0]
    pairs = fibres // 2
    wide = lax.axis_size("wide")
    count = rank_a // SQUARE
    out = jax.ShapeDtypeStruct((count + 1, pairs, LANES), BF16)
    vmem = pl.BlockSpec(memory_space=pltpu.VMEM)
    outside = pl.BlockSpec(memory_space=pltpu.HBM)
    return pl.pallas_call(
        project_kernel,
        out_shape=[out] * SQUARE,
        in_specs=[outside] * 4,
        out_specs=[vmem] * SQUARE,
        scratch_shapes=[
            pltpu.VMEM(blocks.shape, BF16),
            pltpu.VMEM((rank_a, rows), BF16),
            pltpu.VMEM(basis_b.shape, BF16),
            pltpu.VMEM(sketch.shape, BF16),
            pltpu.VMEM((2 * columns, 2 * rank_b), BF16),
            pltpu.VMEM((wide // SQUARE, SQUARE, rank_a // wide, rows), F32),
            pltpu.VMEM((rank_a * pairs, LANES), F32),
            pltpu.SemaphoreType.DMA((3 + len(CUTS),)),
        ],
        compiler_params=pltpu.CompilerParams(vmem_limit_bytes=32 * 2**20),
        name="project",
    )(*(pltpu.with_memory_space_constraint(x, pltpu.HBM) for x in (blocks, basis_a, basis_b, sketch)))


def square_kernel(*refs):
    groups = len(refs) - 5
    moment, own, turned_sketch, gathered, held = refs[groups:]
    _, tiles, pairs, _ = gathered.shape
    count = tiles - 1
    rank = LANES // 2
    wide = lax.axis_index("wide")
    pair = lax.axis_index("pair")
    for k in range(groups):
        gathered[pair ^ k] = refs[k][...]

    def tile(p):
        return gathered[:, p].reshape(groups * pairs, LANES)

    parts = []
    for m in range(count // 2):
        even, odd = tile(2 * m), tile(2 * m + 1)
        first = jnp.concatenate([even[:, :rank], odd[:, :rank]], axis=1)
        second = jnp.concatenate([even[:, rank:], odd[:, rank:]], axis=1)
        parts.append(jnp.concatenate([first, second], axis=0))
    projected = jnp.concatenate(parts, axis=1)
    rides = tile(count).astype(F32)
    omega = jnp.concatenate([rides[:, :rank], rides[:, rank:]], axis=0).T.astype(BF16)
    turned_sketch[...] = omega
    sketched = jnp.dot(omega, projected, preferred_element_type=F32)
    terms = jnp.concatenate(split3(sketched), axis=0)
    product = lax.dot_general(terms, projected, NT, preferred_element_type=F32)
    columns = omega.shape[0]
    moment[...] = product[:columns] + (product[columns : 2 * columns] + product[2 * columns :])
    for m in range(count // 2):
        held[m] = sketched[:, m * LANES : (m + 1) * LANES]
    own[...] = held[lax.div(wide, SQUARE) * groups + pair]


def square_product(*groups):
    tiles, pairs, _ = groups[0].shape
    rank = LANES // 2
    vmem = pl.BlockSpec(memory_space=pltpu.VMEM)
    whole = jax.ShapeDtypeStruct((rank, LANES), F32)
    return pl.pallas_call(
        square_kernel,
        out_shape=[whole, whole, jax.ShapeDtypeStruct((rank, LANES), BF16)],
        in_specs=[vmem] * len(groups),
        out_specs=[vmem] * 3,
        scratch_shapes=[
            pltpu.VMEM((len(groups),) + groups[0].shape, BF16),
            pltpu.VMEM(((tiles - 1) // 2, rank, LANES), F32),
        ],
        compiler_params=pltpu.CompilerParams(vmem_limit_bytes=32 * 2**20),
        name="square_product",
    )(*groups)


def inverse_factor(table):
    rank = table.shape[0]
    tiles = [table[8 * t : 8 * t + 8] for t in range(rank // 8)]
    shape = tiles[0].shape
    below = lax.broadcasted_iota(jnp.int32, shape, 0)
    inverse = []
    for start in range(0, rank, GROUP):
        first, inside = divmod(start, 8)
        last = inside + GROUP == 8
        terms = {
            t: [jnp.broadcast_to(tiles[t][:, start + k : start + k + 1], shape) for k in range(GROUP)]
            for t in range(first, rank // 8)
        }
        lines = [jnp.broadcast_to(tiles[first][inside + k : inside + k + 1], shape) for k in range(GROUP)]
        entry = {
            (k, m): jnp.broadcast_to(terms[first][m][inside + k : inside + k + 1], shape)
            for k in range(GROUP)
            for m in range(k + 1)
        }
        if last:
            del terms[first]
        for k in range(GROUP):
            root = lax.rsqrt(entry[k, k])
            lines[k] = lines[k] * root
            for t in terms:
                terms[t][k] = terms[t][k] * root
            for m in range(k + 1, GROUP):
                entry[m, k] = entry[m, k] * root
            for m in range(k + 1, GROUP):
                for n in range(k + 1, m + 1):
                    entry[m, n] = entry[m, n] - entry[m, k] * entry[n, k]
                lines[m] = lines[m] - entry[m, k] * lines[k]
                for t in terms:
                    terms[t][m] = terms[t][m] - entry[m, k] * terms[t][k]
        for t in terms:
            change = terms[t][0] * lines[0]
            for k in range(1, GROUP):
                change = change + terms[t][k] * lines[k]
            if t == first:
                change = jnp.where(below >= inside + GROUP, change, 0.0)
            tiles[t] = tiles[t] - change
        inverse += [line[:1, rank:] for line in lines]
    return jnp.concatenate(inverse, axis=0)


def finish_kernel(scale, m0, m1, m2, m3, own, turned_sketch, transfer, coefficients):
    wide = lax.axis_index("wide")
    pair = lax.axis_index("pair")
    moment = (m0[...] + m1[...]) + (m2[...] + m3[...])
    rank, fibres = moment.shape
    terms = jnp.concatenate(split3(moment), axis=0)
    product = lax.dot_general(terms, turned_sketch[...], NT, preferred_element_type=F32)
    gram = product[:rank] + (product[rank : 2 * rank] + product[2 * rank :])
    row = lax.broadcasted_iota(jnp.int32, (rank, rank), 0)
    column = lax.broadcasted_iota(jnp.int32, (rank, rank), 1)
    inverse = inverse_factor(jnp.concatenate([gram, (row == column).astype(F32)], axis=1))
    transfer[...] = scale * jnp.dot(
        inverse, own[...], preferred_element_type=F32, precision=lax.Precision.HIGH
    )
    count = coefficients.shape[0]
    groups = lax.axis_size("pair")
    per_group = fibres // groups // 2
    j = lax.broadcasted_iota(jnp.int32, (8, fibres), 0)
    at = lax.rem(j, 2) * (fibres // 2) + pair * per_group + wide * (count // 2) + lax.div(j, 2)
    pick = (lax.broadcasted_iota(jnp.int32, (8, fibres), 1) == at).astype(F32)
    mine = lax.dot_general(pick, moment, NT, preferred_element_type=F32, precision=lax.Precision.HIGHEST)
    found = lax.dot_general(mine, inverse, NT, preferred_element_type=F32, precision=lax.Precision.HIGH)
    coefficients[...] = found[:count]


def finish(moments, own, turned_sketch, scale, count):
    rank = own.shape[0]
    vmem = pl.BlockSpec(memory_space=pltpu.VMEM)
    return pl.pallas_call(
        functools.partial(finish_kernel, scale),
        out_shape=[
            jax.ShapeDtypeStruct(own.shape, F32),
            jax.ShapeDtypeStruct((count, rank), F32),
        ],
        in_specs=[vmem] * 6,
        out_specs=[vmem] * 2,
        compiler_params=pltpu.CompilerParams(vmem_limit_bytes=32 * 2**20),
        name="finish",
    )(*moments, own, turned_sketch)


def partner(x, k):
    return lax.ppermute(x, "wide", [(i, i ^ k) for i in range(lax.axis_size("wide"))])


def beside(x, k, j):
    wide, pair = lax.axis_size("wide"), lax.axis_size("pair")
    pairs = [(i * pair + g, (i ^ k) * pair + (g ^ j)) for i in range(wide) for g in range(pair)]
    return lax.ppermute(x, ("wide", "pair"), pairs)


def in_squares(blocks, basis_a, basis_b, sketch):
    outs = project(blocks, basis_a.T, basis_b.T, sketch)
    got = [partner(outs[k], k) for k in FIRST]
    total = outs[0].astype(F32)
    for term in got:
        total = total + term.astype(F32)
    total = total.astype(BF16)
    other = partner(total, SQUARE)
    total = (total.astype(F32) + other.astype(F32)).astype(BF16)
    across = beside(total, 0, 2)
    near = beside(total, 0, 1)
    groups = [total, near, across, beside(across, 0, 1)]
    moment, own, turned_sketch = square_product(*groups)
    moments = [moment] + [beside(moment, k, 1) for k in SECOND]
    scale = float((basis_a.shape[1] * basis_b.shape[1]) ** 0.5)
    transfer, coefficients = finish(moments, own, turned_sketch, scale, sketch.shape[0])
    return transfer.T, coefficients


def by_columns(blocks, basis_a, basis_b, sketch):
    rank_a, rank_b = basis_a.shape[1], basis_b.shape[1]
    rows = blocks.shape[1]
    wide, pair = lax.axis_size("wide"), lax.axis_size("pair")
    narrowed = jnp.einsum("fac,cr->far", blocks, basis_b, preferred_element_type=F32).astype(BF16)
    own_rows = lax.dynamic_slice_in_dim(basis_a, lax.axis_index("wide") * rows, rows, 0)
    part = jnp.einsum("ap,far->fpr", own_rows, narrowed, preferred_element_type=F32).astype(BF16)
    fibres = part.shape[0]
    part = part.reshape(fibres, wide * pair, -1).swapaxes(0, 1)
    part = lax.all_to_all(part, ("wide", "pair"), 0, 0, tiled=True)
    part = part.reshape(wide, pair * fibres, -1).astype(F32).sum(0)
    omega = lax.all_gather(sketch, ("pair", "wide"), tiled=True).astype(F32)
    exact = functools.partial(jnp.dot, precision=lax.Precision.HIGHEST)
    own = exact(part.T, omega)
    moment = lax.psum(exact(part, own), ("wide", "pair"))
    lower = jnp.linalg.cholesky(exact(omega.T, moment))
    solve = functools.partial(
        lax.linalg.triangular_solve, lower, left_side=False, lower=True, transpose_a=True
    )
    count = sketch.shape[0]
    mine = lax.dynamic_slice_in_dim(moment, lax.axis_index(("pair", "wide")) * count, count, 0)
    return solve(own) * jnp.sqrt(F32(rank_a * rank_b)), solve(mine)


def solution(mesh):
    placed = (P("pair", "wide", None), P(), P(), P(("pair", "wide"), None))

    def per_device(blocks, basis_a, basis_b, sketch):
        fibres, rows, _ = blocks.shape
        rank_a, rank_b = basis_a.shape[1], basis_b.shape[1]
        wide, pair = lax.axis_size("wide"), lax.axis_size("pair")
        fits = (
            wide == 2 * SQUARE
            and rank_b == LANES // 2
            and sketch.shape[1] == LANES // 2
            and rank_a == 2 * wide * pair
            and rows == LANES
            and fibres * pair == LANES
            and fibres % 32 == 0
        )
        return (in_squares if fits else by_columns)(blocks, basis_a, basis_b, sketch)

    return jax.shard_map(
        per_device,
        mesh=mesh,
        in_specs=placed,
        out_specs=(P(("wide", "pair"), None), P(("pair", "wide"), None)),
        check_vma=False,
    )
```

```python
import functools

import jax
import jax.numpy as jnp
from jax import lax
from jax.experimental import pallas as pl
from jax.experimental.pallas import tpu as pltpu
from jax.sharding import PartitionSpec as P

F32 = jnp.float32
BF16 = jnp.bfloat16
LANES = 128
SQUARE = 4
CUTS = (2, 2, 2, 2)
SPLIT = 2
FIRST = (3, 2, 1)
SECOND = (1, 2, 3)
GROUP = 8
NT = (((1,), (1,)), ((), ()))


def split3(x):
    high = x.astype(BF16)
    rest = x - high.astype(F32)
    middle = rest.astype(BF16)
    low = (rest - middle.astype(F32)).astype(BF16)
    return high, middle, low


def project_kernel(blocks, basis_a, basis_b, sketch, *refs):
    outs = refs[:SQUARE]
    held, rows_a, held_b, held_s, diagonal, wanted, sums, sems = refs[SQUARE:]
    wide = lax.axis_index("wide")
    fibres, rows, columns = blocks.shape
    rank_b = basis_b.shape[0]
    rank_a = basis_a.shape[0]
    pairs = fibres // 2
    small = [
        pltpu.make_async_copy(basis_b, held_b, sems.at[0]),
        pltpu.make_async_copy(basis_a.at[:, pl.ds(pl.multiple_of(wide * rows, rows), rows)], rows_a, sems.at[1]),
        pltpu.make_async_copy(sketch, held_s, sems.at[2]),
    ]
    unit = fibres // sum(CUTS)
    parts, begin = [], 0
    for cut in CUTS:
        parts.append((begin, cut * unit))
        begin += cut * unit
    large = [
        pltpu.make_async_copy(blocks.at[pl.ds(at, n)], held.at[pl.ds(at, n)], sems.at[3 + i])
        for i, (at, n) in enumerate(parts)
    ]
    for copy in small + large:
        copy.start()
    small[0].wait()
    basis = held_b[...].astype(F32).T.astype(BF16)
    empty = jnp.zeros_like(basis)
    diagonal[pl.ds(0, columns)] = jnp.concatenate([basis, empty], axis=1)
    diagonal[pl.ds(columns, columns)] = jnp.concatenate([empty, basis], axis=1)
    small[1].wait()
    wanted[...] = rows_a[...].astype(F32).reshape(wanted.shape)
    square = lax.rem(wide, SQUARE)
    halves = wanted.shape[0]
    left = jnp.concatenate(
        [wanted[half, square ^ k] for k in range(SQUARE) for half in range(halves)], axis=0
    ).astype(BF16)

    def narrow(at, n):
        found = []
        for i in range(SPLIT):
            here = held[pl.ds(at + i * n // SPLIT, n // SPLIT)].reshape(n // SPLIT // 2, 2, rows, columns)
            lhs = jnp.concatenate([here[:, j].reshape(-1, columns) for j in range(2)], axis=1)
            found.append(jnp.dot(lhs, diagonal[...], preferred_element_type=F32).astype(BF16))
        return jnp.concatenate(found, axis=0)

    def fold(at, n, narrowed):
        for q in range(n // 4):
            two = [narrowed[(2 * q + t) * rows : (2 * q + t + 1) * rows] for t in range(2)]
            found = jnp.dot(left, jnp.concatenate(two, axis=1), preferred_element_type=F32)
            for t in range(2):
                sums[pl.ds(at // 2 + 2 * q + t, rank_a, stride=pairs), :] = found[:, t * LANES : (t + 1) * LANES]

    late = None
    for copy, (at, n) in zip(large, parts):
        copy.wait()
        narrowed = narrow(at, n)
        if late is not None:
            fold(*late)
        late = (at, n, narrowed)
    fold(*late)
    small[2].wait()
    mine = held_s[...].astype(F32)
    own = mine.shape[0]
    row = lax.broadcasted_iota(jnp.int32, (pairs, LANES), 0)
    tile = jnp.zeros((pairs, LANES), F32)
    for j in range(own // 2):
        line = jnp.concatenate([mine[2 * j : 2 * j + 1], mine[2 * j + 1 : 2 * j + 2]], axis=1)
        tile = jnp.where(row == wide * (own // 2) + j, line, tile)
    count = rank_a // SQUARE
    for k in range(SQUARE):
        found = sums[pl.ds(k * count * pairs, count * pairs), :].reshape(count, pairs, LANES)
        outs[k][pl.ds(0, count)] = found.astype(outs[k].dtype)
        outs[k][count] = tile.astype(outs[k].dtype)


def project(blocks, basis_a, basis_b, sketch):
    fibres, rows, columns = blocks.shape
    rank_a = basis_a.shape[0]
    rank_b = basis_b.shape[0]
    pairs = fibres // 2
    wide = lax.axis_size("wide")
    count = rank_a // SQUARE
    shape = (count + 1, pairs, LANES)
    out = [jax.ShapeDtypeStruct(shape, F32 if k == 0 else BF16) for k in range(SQUARE)]
    vmem = pl.BlockSpec(memory_space=pltpu.VMEM)
    outside = pl.BlockSpec(memory_space=pltpu.HBM)
    return pl.pallas_call(
        project_kernel,
        out_shape=out,
        in_specs=[outside] * 4,
        out_specs=[vmem] * SQUARE,
        scratch_shapes=[
            pltpu.VMEM(blocks.shape, BF16),
            pltpu.VMEM((rank_a, rows), BF16),
            pltpu.VMEM(basis_b.shape, BF16),
            pltpu.VMEM(sketch.shape, BF16),
            pltpu.VMEM((2 * columns, 2 * rank_b), BF16),
            pltpu.VMEM((wide // SQUARE, SQUARE, rank_a // wide, rows), F32),
            pltpu.VMEM((rank_a * pairs + pairs, LANES), F32),
            pltpu.SemaphoreType.DMA((3 + len(CUTS),)),
        ],
        compiler_params=pltpu.CompilerParams(vmem_limit_bytes=32 * 2**20),
        name="project",
    )(*(pltpu.with_memory_space_constraint(x, pltpu.HBM) for x in (blocks, basis_a, basis_b, sketch)))


def square_kernel(*refs):
    groups = len(refs) - 5
    moment, own, turned_sketch, gathered, held = refs[groups:]
    _, tiles, pairs, _ = gathered.shape
    count = tiles - 1
    rank = LANES // 2
    wide = lax.axis_index("wide")
    pair = lax.axis_index("pair")
    for k in range(groups):
        gathered[pair ^ k] = refs[k][...]

    def tile(p):
        return gathered[:, p].reshape(groups * pairs, LANES)

    parts = []
    for m in range(count // 2):
        even, odd = tile(2 * m), tile(2 * m + 1)
        first = jnp.concatenate([even[:, :rank], odd[:, :rank]], axis=1)
        second = jnp.concatenate([even[:, rank:], odd[:, rank:]], axis=1)
        parts.append(jnp.concatenate([first, second], axis=0))
    projected = jnp.concatenate(parts, axis=1)
    rides = tile(count).astype(F32)
    omega = jnp.concatenate([rides[:, :rank], rides[:, rank:]], axis=0).T.astype(BF16)
    turned_sketch[...] = omega
    sketched = jnp.dot(omega, projected, preferred_element_type=F32)
    terms = jnp.concatenate(split3(sketched), axis=0)
    product = lax.dot_general(terms, projected, NT, preferred_element_type=F32)
    columns = omega.shape[0]
    moment[...] = product[:columns] + (product[columns : 2 * columns] + product[2 * columns :])
    for m in range(count // 2):
        held[m] = sketched[:, m * LANES : (m + 1) * LANES]
    own[...] = held[lax.div(wide, SQUARE) * groups + pair]


def square_product(*groups):
    tiles, pairs, _ = groups[0].shape
    rank = LANES // 2
    vmem = pl.BlockSpec(memory_space=pltpu.VMEM)
    whole = jax.ShapeDtypeStruct((rank, LANES), F32)
    return pl.pallas_call(
        square_kernel,
        out_shape=[whole, whole, jax.ShapeDtypeStruct((rank, LANES), BF16)],
        in_specs=[vmem] * len(groups),
        out_specs=[vmem] * 3,
        scratch_shapes=[
            pltpu.VMEM((len(groups),) + groups[0].shape, BF16),
            pltpu.VMEM(((tiles - 1) // 2, rank, LANES), F32),
        ],
        compiler_params=pltpu.CompilerParams(vmem_limit_bytes=32 * 2**20),
        name="square_product",
    )(*groups)


def inverse_factor(table):
    rank = table.shape[0]
    tiles = [table[8 * t : 8 * t + 8] for t in range(rank // 8)]
    shape = tiles[0].shape
    below = lax.broadcasted_iota(jnp.int32, shape, 0)
    inverse = []
    for start in range(0, rank, GROUP):
        first, inside = divmod(start, 8)
        last = inside + GROUP == 8
        terms = {
            t: [jnp.broadcast_to(tiles[t][:, start + k : start + k + 1], shape) for k in range(GROUP)]
            for t in range(first, rank // 8)
        }
        lines = [jnp.broadcast_to(tiles[first][inside + k : inside + k + 1], shape) for k in range(GROUP)]
        entry = {
            (k, m): jnp.broadcast_to(terms[first][m][inside + k : inside + k + 1], shape)
            for k in range(GROUP)
            for m in range(k + 1)
        }
        if last:
            del terms[first]
        for k in range(GROUP):
            root = lax.rsqrt(entry[k, k])
            lines[k] = lines[k] * root
            for t in terms:
                terms[t][k] = terms[t][k] * root
            for m in range(k + 1, GROUP):
                entry[m, k] = entry[m, k] * root
            for m in range(k + 1, GROUP):
                for n in range(k + 1, m + 1):
                    entry[m, n] = entry[m, n] - entry[m, k] * entry[n, k]
                lines[m] = lines[m] - entry[m, k] * lines[k]
                for t in terms:
                    terms[t][m] = terms[t][m] - entry[m, k] * terms[t][k]
        for t in terms:
            change = terms[t][0] * lines[0]
            for k in range(1, GROUP):
                change = change + terms[t][k] * lines[k]
            if t == first:
                change = jnp.where(below >= inside + GROUP, change, 0.0)
            tiles[t] = tiles[t] - change
        inverse += [line[:1, rank:] for line in lines]
    return jnp.concatenate(inverse, axis=0)


def finish_kernel(scale, m0, m1, m2, m3, own, turned_sketch, transfer, coefficients):
    wide = lax.axis_index("wide")
    pair = lax.axis_index("pair")
    moment = (m0[...] + m1[...]) + (m2[...] + m3[...])
    rank, fibres = moment.shape
    terms = jnp.concatenate(split3(moment), axis=0)
    product = lax.dot_general(terms, turned_sketch[...], NT, preferred_element_type=F32)
    gram = product[:rank] + (product[rank : 2 * rank] + product[2 * rank :])
    row = lax.broadcasted_iota(jnp.int32, (rank, rank), 0)
    column = lax.broadcasted_iota(jnp.int32, (rank, rank), 1)
    inverse = inverse_factor(jnp.concatenate([gram, (row == column).astype(F32)], axis=1))
    transfer[...] = scale * jnp.dot(
        inverse, own[...], preferred_element_type=F32, precision=lax.Precision.HIGH
    )
    count = coefficients.shape[0]
    groups = lax.axis_size("pair")
    per_group = fibres // groups // 2
    j = lax.broadcasted_iota(jnp.int32, (8, fibres), 0)
    at = lax.rem(j, 2) * (fibres // 2) + pair * per_group + wide * (count // 2) + lax.div(j, 2)
    pick = (lax.broadcasted_iota(jnp.int32, (8, fibres), 1) == at).astype(F32)
    mine = lax.dot_general(pick, moment, NT, preferred_element_type=F32, precision=lax.Precision.HIGHEST)
    found = lax.dot_general(mine, inverse, NT, preferred_element_type=F32, precision=lax.Precision.HIGH)
    coefficients[...] = found[:count]


def finish(moments, own, turned_sketch, scale, count):
    rank = own.shape[0]
    vmem = pl.BlockSpec(memory_space=pltpu.VMEM)
    return pl.pallas_call(
        functools.partial(finish_kernel, scale),
        out_shape=[
            jax.ShapeDtypeStruct(own.shape, F32),
            jax.ShapeDtypeStruct((count, rank), F32),
        ],
        in_specs=[vmem] * 6,
        out_specs=[vmem] * 2,
        compiler_params=pltpu.CompilerParams(vmem_limit_bytes=32 * 2**20),
        name="finish",
    )(*moments, own, turned_sketch)


def partner(x, k):
    return lax.ppermute(x, "wide", [(i, i ^ k) for i in range(lax.axis_size("wide"))])


def beside(x, k, j):
    wide, pair = lax.axis_size("wide"), lax.axis_size("pair")
    pairs = [(i * pair + g, (i ^ k) * pair + (g ^ j)) for i in range(wide) for g in range(pair)]
    return lax.ppermute(x, ("wide", "pair"), pairs)


def in_squares(blocks, basis_a, basis_b, sketch):
    outs = project(blocks, basis_a.T, basis_b.T, sketch)
    got = [partner(outs[k], k) for k in FIRST]
    total = outs[0]
    for term in got:
        total = total + term.astype(F32)
    total = total.astype(BF16)
    other = partner(total, SQUARE)
    total = (total.astype(F32) + other.astype(F32)).astype(BF16)
    across = beside(total, 0, 2)
    near = beside(total, 0, 1)
    groups = [total, near, across, beside(across, 0, 1)]
    moment, own, turned_sketch = square_product(*groups)
    moments = [moment] + [beside(moment, k, 1) for k in SECOND]
    scale = float((basis_a.shape[1] * basis_b.shape[1]) ** 0.5)
    transfer, coefficients = finish(moments, own, turned_sketch, scale, sketch.shape[0])
    return transfer.T, coefficients


def by_columns(blocks, basis_a, basis_b, sketch):
    rank_a, rank_b = basis_a.shape[1], basis_b.shape[1]
    rows = blocks.shape[1]
    wide, pair = lax.axis_size("wide"), lax.axis_size("pair")
    narrowed = jnp.einsum("fac,cr->far", blocks, basis_b, preferred_element_type=F32).astype(BF16)
    own_rows = lax.dynamic_slice_in_dim(basis_a, lax.axis_index("wide") * rows, rows, 0)
    part = jnp.einsum("ap,far->fpr", own_rows, narrowed, preferred_element_type=F32).astype(BF16)
    fibres = part.shape[0]
    part = part.reshape(fibres, wide * pair, -1).swapaxes(0, 1)
    part = lax.all_to_all(part, ("wide", "pair"), 0, 0, tiled=True)
    part = part.reshape(wide, pair * fibres, -1).astype(F32).sum(0)
    omega = lax.all_gather(sketch, ("pair", "wide"), tiled=True).astype(F32)
    exact = functools.partial(jnp.dot, precision=lax.Precision.HIGHEST)
    own = exact(part.T, omega)
    moment = lax.psum(exact(part, own), ("wide", "pair"))
    lower = jnp.linalg.cholesky(exact(omega.T, moment))
    solve = functools.partial(
        lax.linalg.triangular_solve, lower, left_side=False, lower=True, transpose_a=True
    )
    count = sketch.shape[0]
    mine = lax.dynamic_slice_in_dim(moment, lax.axis_index(("pair", "wide")) * count, count, 0)
    return solve(own) * jnp.sqrt(F32(rank_a * rank_b)), solve(mine)


def solution(mesh):
    placed = (P("pair", "wide", None), P(), P(), P(("pair", "wide"), None))

    def per_device(blocks, basis_a, basis_b, sketch):
        fibres, rows, _ = blocks.shape
        rank_a, rank_b = basis_a.shape[1], basis_b.shape[1]
        wide, pair = lax.axis_size("wide"), lax.axis_size("pair")
        fits = (
            wide == 2 * SQUARE
            and rank_b == LANES // 2
            and sketch.shape[1] == LANES // 2
            and rank_a == 2 * wide * pair
            and rows == LANES
            and fibres * pair == LANES
            and fibres % 32 == 0
        )
        return (in_squares if fits else by_columns)(blocks, basis_a, basis_b, sketch)

    return jax.shard_map(
        per_device,
        mesh=mesh,
        in_specs=placed,
        out_specs=(P(("wide", "pair"), None), P(("pair", "wide"), None)),
        check_vma=False,
    )
```

```python
import functools

import jax
import jax.numpy as jnp
from jax import lax
from jax.experimental import pallas as pl
from jax.experimental.pallas import tpu as pltpu
from jax.sharding import PartitionSpec as P

F32 = jnp.float32
BF16 = jnp.bfloat16
LANES = 128
SQUARE = 4
CUTS = (2, 2, 2, 2)
SPLIT = 2
FIRST = (3, 2, 1)
SECOND = (1, 2, 3)
GROUP = 8
NT = (((1,), (1,)), ((), ()))


def split3(x):
    high = x.astype(BF16)
    rest = x - high.astype(F32)
    middle = rest.astype(BF16)
    low = (rest - middle.astype(F32)).astype(BF16)
    return high, middle, low


def project_kernel(blocks, basis_a, basis_b, sketch, *refs):
    outs = refs[:SQUARE]
    held, rows_a, held_b, held_s, diagonal, wanted, sums, sems = refs[SQUARE:]
    wide = lax.axis_index("wide")
    fibres, rows, columns = blocks.shape
    rank_b = basis_b.shape[0]
    rank_a = basis_a.shape[0]
    pairs = fibres // 2
    small = [
        pltpu.make_async_copy(basis_b, held_b, sems.at[0]),
        pltpu.make_async_copy(basis_a.at[:, pl.ds(pl.multiple_of(wide * rows, rows), rows)], rows_a, sems.at[1]),
        pltpu.make_async_copy(sketch, held_s, sems.at[2]),
    ]
    unit = fibres // sum(CUTS)
    parts, begin = [], 0
    for cut in CUTS:
        parts.append((begin, cut * unit))
        begin += cut * unit
    large = [
        pltpu.make_async_copy(blocks.at[pl.ds(at, n)], held.at[pl.ds(at, n)], sems.at[3 + i])
        for i, (at, n) in enumerate(parts)
    ]
    for copy in small + large:
        copy.start()
    small[0].wait()
    basis = held_b[...].astype(F32).T.astype(BF16)
    empty = jnp.zeros_like(basis)
    diagonal[pl.ds(0, columns)] = jnp.concatenate([basis, empty], axis=1)
    diagonal[pl.ds(columns, columns)] = jnp.concatenate([empty, basis], axis=1)
    small[1].wait()
    wanted[...] = rows_a[...].astype(F32).reshape(wanted.shape)
    square = lax.rem(wide, SQUARE)
    halves = wanted.shape[0]
    left = jnp.concatenate(
        [wanted[half, square ^ k] for k in range(SQUARE) for half in range(halves)], axis=0
    ).astype(BF16)

    def narrow(at, n):
        found = []
        for i in range(SPLIT):
            here = held[pl.ds(at + i * n // SPLIT, n // SPLIT)].reshape(n // SPLIT // 2, 2, rows, columns)
            lhs = jnp.concatenate([here[:, j].reshape(-1, columns) for j in range(2)], axis=1)
            found.append(jnp.dot(lhs, diagonal[...], preferred_element_type=F32).astype(BF16))
        return jnp.concatenate(found, axis=0)

    def fold(at, n, narrowed):
        for q in range(n // 4):
            two = [narrowed[(2 * q + t) * rows : (2 * q + t + 1) * rows] for t in range(2)]
            found = jnp.dot(left, jnp.concatenate(two, axis=1), preferred_element_type=F32)
            for t in range(2):
                sums[pl.ds(at // 2 + 2 * q + t, rank_a, stride=pairs), :] = found[:, t * LANES : (t + 1) * LANES]

    late = None
    for copy, (at, n) in zip(large, parts):
        copy.wait()
        narrowed = narrow(at, n)
        if late is not None:
            fold(*late)
        late = (at, n, narrowed)
    fold(*late)
    small[2].wait()
    mine = held_s[...].astype(F32)
    own = mine.shape[0]
    row = lax.broadcasted_iota(jnp.int32, (pairs, LANES), 0)
    tile = jnp.zeros((pairs, LANES), F32)
    for j in range(own // 2):
        line = jnp.concatenate([mine[2 * j : 2 * j + 1], mine[2 * j + 1 : 2 * j + 2]], axis=1)
        tile = jnp.where(row == wide * (own // 2) + j, line, tile)
    count = rank_a // SQUARE
    for k in range(SQUARE):
        found = sums[pl.ds(k * count * pairs, count * pairs), :].reshape(count, pairs, LANES)
        outs[k][pl.ds(0, count)] = found.astype(outs[k].dtype)
        outs[k][count] = tile.astype(outs[k].dtype)


def project(blocks, basis_a, basis_b, sketch):
    fibres, rows, columns = blocks.shape
    rank_a = basis_a.shape[0]
    rank_b = basis_b.shape[0]
    pairs = fibres // 2
    wide = lax.axis_size("wide")
    count = rank_a // SQUARE
    shape = (count + 1, pairs, LANES)
    out = [jax.ShapeDtypeStruct(shape, F32 if k == 0 else BF16) for k in range(SQUARE)]
    vmem = pl.BlockSpec(memory_space=pltpu.VMEM)
    outside = pl.BlockSpec(memory_space=pltpu.HBM)
    return pl.pallas_call(
        project_kernel,
        out_shape=out,
        in_specs=[outside] * 4,
        out_specs=[vmem] * SQUARE,
        scratch_shapes=[
            pltpu.VMEM(blocks.shape, BF16),
            pltpu.VMEM((rank_a, rows), BF16),
            pltpu.VMEM(basis_b.shape, BF16),
            pltpu.VMEM(sketch.shape, BF16),
            pltpu.VMEM((2 * columns, 2 * rank_b), BF16),
            pltpu.VMEM((wide // SQUARE, SQUARE, rank_a // wide, rows), F32),
            pltpu.VMEM((rank_a * pairs + pairs, LANES), F32),
            pltpu.SemaphoreType.DMA((3 + len(CUTS),)),
        ],
        compiler_params=pltpu.CompilerParams(vmem_limit_bytes=32 * 2**20),
        name="project",
    )(*(pltpu.with_memory_space_constraint(x, pltpu.HBM) for x in (blocks, basis_a, basis_b, sketch)))


def square_kernel(*refs):
    groups = len(refs) - 5
    moment, own, turned_sketch, gathered, held = refs[groups:]
    _, tiles, pairs, _ = gathered.shape
    count = tiles - 1
    rank = LANES // 2
    wide = lax.axis_index("wide")
    pair = lax.axis_index("pair")
    for k in range(groups):
        gathered[pair ^ k] = refs[k][...]

    def tile(p):
        return gathered[:, p].reshape(groups * pairs, LANES)

    parts = []
    for m in range(count // 2):
        even, odd = tile(2 * m), tile(2 * m + 1)
        first = jnp.concatenate([even[:, :rank], odd[:, :rank]], axis=1)
        second = jnp.concatenate([even[:, rank:], odd[:, rank:]], axis=1)
        parts.append(jnp.concatenate([first, second], axis=0))
    projected = jnp.concatenate(parts, axis=1)
    rides = tile(count).astype(F32)
    omega = jnp.concatenate([rides[:, :rank], rides[:, rank:]], axis=0).T.astype(BF16)
    turned_sketch[...] = omega
    sketched = jnp.dot(omega, projected, preferred_element_type=F32)
    terms = jnp.concatenate(split3(sketched), axis=0)
    product = lax.dot_general(terms, projected, NT, preferred_element_type=F32)
    columns = omega.shape[0]
    moment[...] = product[:columns] + (product[columns : 2 * columns] + product[2 * columns :])
    for m in range(count // 2):
        held[m] = sketched[:, m * LANES : (m + 1) * LANES]
    own[...] = held[lax.div(wide, SQUARE) * groups + pair]


def square_product(*groups):
    tiles, pairs, _ = groups[0].shape
    rank = LANES // 2
    vmem = pl.BlockSpec(memory_space=pltpu.VMEM)
    whole = jax.ShapeDtypeStruct((rank, LANES), F32)
    return pl.pallas_call(
        square_kernel,
        out_shape=[whole, whole, jax.ShapeDtypeStruct((rank, LANES), BF16)],
        in_specs=[vmem] * len(groups),
        out_specs=[vmem] * 3,
        scratch_shapes=[
            pltpu.VMEM((len(groups),) + groups[0].shape, BF16),
            pltpu.VMEM(((tiles - 1) // 2, rank, LANES), F32),
        ],
        compiler_params=pltpu.CompilerParams(vmem_limit_bytes=32 * 2**20),
        name="square_product",
    )(*groups)


def inverse_factor(table):
    rank = table.shape[0]
    tiles = [table[8 * t : 8 * t + 8] for t in range(rank // 8)]
    shape = tiles[0].shape
    below = lax.broadcasted_iota(jnp.int32, shape, 0)
    inverse = []
    for start in range(0, rank, GROUP):
        first, inside = divmod(start, 8)
        last = inside + GROUP == 8
        terms = {
            t: [jnp.broadcast_to(tiles[t][:, start + k : start + k + 1], shape) for k in range(GROUP)]
            for t in range(first, rank // 8)
        }
        lines = [jnp.broadcast_to(tiles[first][inside + k : inside + k + 1], shape) for k in range(GROUP)]
        entry = {
            (k, m): jnp.broadcast_to(terms[first][m][inside + k : inside + k + 1], shape)
            for k in range(GROUP)
            for m in range(k + 1)
        }
        if last:
            del terms[first]
        for k in range(GROUP):
            root = lax.rsqrt(entry[k, k])
            lines[k] = lines[k] * root
            for t in terms:
                terms[t][k] = terms[t][k] * root
            for m in range(k + 1, GROUP):
                entry[m, k] = entry[m, k] * root
            for m in range(k + 1, GROUP):
                for n in range(k + 1, m + 1):
                    entry[m, n] = entry[m, n] - entry[m, k] * entry[n, k]
                lines[m] = lines[m] - entry[m, k] * lines[k]
                for t in terms:
                    terms[t][m] = terms[t][m] - entry[m, k] * terms[t][k]
        for t in terms:
            change = terms[t][0] * lines[0]
            for k in range(1, GROUP):
                change = change + terms[t][k] * lines[k]
            if t == first:
                change = jnp.where(below >= inside + GROUP, change, 0.0)
            tiles[t] = tiles[t] - change
        inverse += [line[:1, rank:] for line in lines]
    return jnp.concatenate(inverse, axis=0)


def finish_kernel(scale, m0, m1, m2, m3, own, turned_sketch, transfer, coefficients):
    wide = lax.axis_index("wide")
    pair = lax.axis_index("pair")
    moment = (m0[...] + m1[...]) + (m2[...] + m3[...])
    rank, fibres = moment.shape
    terms = jnp.concatenate(split3(moment), axis=0)
    product = lax.dot_general(terms, turned_sketch[...], NT, preferred_element_type=F32)
    gram = product[:rank] + (product[rank : 2 * rank] + product[2 * rank :])
    row = lax.broadcasted_iota(jnp.int32, (rank, rank), 0)
    column = lax.broadcasted_iota(jnp.int32, (rank, rank), 1)
    inverse = inverse_factor(jnp.concatenate([gram, (row == column).astype(F32)], axis=1))
    transfer[...] = scale * jnp.dot(
        inverse, own[...], preferred_element_type=F32, precision=lax.Precision.HIGH
    )
    count = coefficients.shape[0]
    groups = lax.axis_size("pair")
    per_group = fibres // groups // 2
    j = lax.broadcasted_iota(jnp.int32, (8, fibres), 0)
    at = lax.rem(j, 2) * (fibres // 2) + pair * per_group + wide * (count // 2) + lax.div(j, 2)
    pick = (lax.broadcasted_iota(jnp.int32, (8, fibres), 1) == at).astype(F32)
    mine = lax.dot_general(pick, moment, NT, preferred_element_type=F32, precision=lax.Precision.HIGHEST)
    found = lax.dot_general(mine, inverse, NT, preferred_element_type=F32, precision=lax.Precision.HIGH)
    coefficients[...] = found[:count]


def finish(moments, own, turned_sketch, scale, count):
    rank = own.shape[0]
    vmem = pl.BlockSpec(memory_space=pltpu.VMEM)
    return pl.pallas_call(
        functools.partial(finish_kernel, scale),
        out_shape=[
            jax.ShapeDtypeStruct(own.shape, F32),
            jax.ShapeDtypeStruct((count, rank), F32),
        ],
        in_specs=[vmem] * 6,
        out_specs=[vmem] * 2,
        compiler_params=pltpu.CompilerParams(vmem_limit_bytes=32 * 2**20),
        name="finish",
    )(*moments, own, turned_sketch)


def partner(x, k):
    return lax.ppermute(x, "wide", [(i, i ^ k) for i in range(lax.axis_size("wide"))])


def beside(x, k, j):
    wide, pair = lax.axis_size("wide"), lax.axis_size("pair")
    pairs = [(i * pair + g, (i ^ k) * pair + (g ^ j)) for i in range(wide) for g in range(pair)]
    return lax.ppermute(x, ("wide", "pair"), pairs)


def in_squares(blocks, basis_a, basis_b, sketch):
    outs = project(blocks, basis_a.T, basis_b.T, sketch)
    got = [partner(outs[k], k) for k in FIRST]
    total = outs[0]
    for term in got:
        total = total + term.astype(F32)
    total = total.astype(BF16)
    above = beside(total, SQUARE, 0)
    both = beside(total, SQUARE, 2)
    level = beside(total, 0, 2)
    here = (total.astype(F32) + above.astype(F32)).astype(BF16)
    across = (level.astype(F32) + both.astype(F32)).astype(BF16)
    groups = [here, beside(here, 0, 1), across, beside(across, 0, 1)]
    moment, own, turned_sketch = square_product(*groups)
    moments = [moment] + [beside(moment, k, 1) for k in SECOND]
    scale = float((basis_a.shape[1] * basis_b.shape[1]) ** 0.5)
    transfer, coefficients = finish(moments, own, turned_sketch, scale, sketch.shape[0])
    return transfer.T, coefficients


def by_columns(blocks, basis_a, basis_b, sketch):
    rank_a, rank_b = basis_a.shape[1], basis_b.shape[1]
    rows = blocks.shape[1]
    wide, pair = lax.axis_size("wide"), lax.axis_size("pair")
    narrowed = jnp.einsum("fac,cr->far", blocks, basis_b, preferred_element_type=F32).astype(BF16)
    own_rows = lax.dynamic_slice_in_dim(basis_a, lax.axis_index("wide") * rows, rows, 0)
    part = jnp.einsum("ap,far->fpr", own_rows, narrowed, preferred_element_type=F32).astype(BF16)
    fibres = part.shape[0]
    part = part.reshape(fibres, wide * pair, -1).swapaxes(0, 1)
    part = lax.all_to_all(part, ("wide", "pair"), 0, 0, tiled=True)
    part = part.reshape(wide, pair * fibres, -1).astype(F32).sum(0)
    omega = lax.all_gather(sketch, ("pair", "wide"), tiled=True).astype(F32)
    exact = functools.partial(jnp.dot, precision=lax.Precision.HIGHEST)
    own = exact(part.T, omega)
    moment = lax.psum(exact(part, own), ("wide", "pair"))
    lower = jnp.linalg.cholesky(exact(omega.T, moment))
    solve = functools.partial(
        lax.linalg.triangular_solve, lower, left_side=False, lower=True, transpose_a=True
    )
    count = sketch.shape[0]
    mine = lax.dynamic_slice_in_dim(moment, lax.axis_index(("pair", "wide")) * count, count, 0)
    return solve(own) * jnp.sqrt(F32(rank_a * rank_b)), solve(mine)


def solution(mesh):
    placed = (P("pair", "wide", None), P(), P(), P(("pair", "wide"), None))

    def per_device(blocks, basis_a, basis_b, sketch):
        fibres, rows, _ = blocks.shape
        rank_a, rank_b = basis_a.shape[1], basis_b.shape[1]
        wide, pair = lax.axis_size("wide"), lax.axis_size("pair")
        fits = (
            wide == 2 * SQUARE
            and rank_b == LANES // 2
            and sketch.shape[1] == LANES // 2
            and rank_a == 2 * wide * pair
            and rows == LANES
            and fibres * pair == LANES
            and fibres % 32 == 0
        )
        return (in_squares if fits else by_columns)(blocks, basis_a, basis_b, sketch)

    return jax.shard_map(
        per_device,
        mesh=mesh,
        in_specs=placed,
        out_specs=(P(("wide", "pair"), None), P(("pair", "wide"), None)),
        check_vma=False,
    )
```
